32 devices in a mesh: ctx: 8 (over y, x, core), head: 4 (over z).
Axes of the slice: x: 2, y: 2, z: 4, core: 2. Of those that a mesh axis runs over, the one named last changes fastest.
Arguments:
- queries: bfloat16 [4096, 4096], P('ctx', 'head'), may hold values from -150 to 150
- cached_keys: bfloat16 [4096, 2048], P('ctx', 'head'), may hold values from -6 to 6
- values: bfloat16 [4096, 2048], P('ctx', 'head'), may hold values from -6 to 6
- patch_keys: bfloat16 [4096, 2048], P('ctx', 'head'), may hold values from -6 to 6
- out_grad: bfloat16 [4096, 5376], P('ctx', 'head'), may hold values from -6 to 6
- out_weight: bfloat16 [4096, 5376], P('head'), may hold values from -0.09375 to 0.09375
- knocked: int32 [16], P('head'), may hold values 0 or 1
- patch_start: int32 [16], P('head'), may hold values from 0 to 4095
Outputs:
- query_grad: bfloat16 [4096, 4096], P('ctx', 'head')
- key_grad: bfloat16 [4096, 2048], P('ctx', 'head')
- value_grad: bfloat16 [4096, 2048], P('ctx', 'head')
- patch_grad: bfloat16 [4096, 2048], P('ctx', 'head')
- weight_grad: float32 [4096, 5376], P(('head', 'ctx'))
The draws below stay inside these ranges and needn't reach their ends.
All inputs are finite; a program needn't handle non-finite values. No bound on the sum of `knocked` on one device may be relied on, other than what follows from the above.
Results may differ from the reference program's by a relative error of at most 0.0058.
Values may be sent and summed in bfloat16 or wider, within the bound.
No kernel may reach another device: no remote copies, remote signals or barrier semaphores. Data moves between devices by JAX's collectives and lax.ppermute only.
A program may use at most 128 MiB of HBM per device.

```python
import jax
import jax.numpy as jnp
from jax import lax

MODEL = 5376
QH = 32
KVH = 16
HEAD_DIM = 128
WINDOW = 1024
TOK_DEV = 512
TOKENS = 4096


def key_base(key):
    return jnp.clip(jax.random.normal(jax.random.fold_in(key, 11), (TOKENS, KVH * HEAD_DIM), jnp.float32), -6.0, 6.0)


def draw_cached_keys(key, part):
    return key_base(key).astype(jnp.bfloat16)


def draw_queries(key, part):
    base = jnp.clip(jax.random.normal(jax.random.fold_in(key, 12), (TOKENS, QH * HEAD_DIM), jnp.float32), -6.0, 6.0)
    return base.astype(jnp.bfloat16)


def touch_ends(result, rng, low, high):
    index_at = [jax.random.randint(jax.random.fold_in(rng, axis), (), 0, length) for axis, length in enumerate(result.shape)]
    longest = result.shape.index(max(result.shape))
    next_to = index_at[:longest] + [(index_at[longest] + 1) % result.shape[longest]] + index_at[longest + 1:]
    return result.at[tuple(index_at)].set(low).at[tuple(next_to)].set(high)


def levels(rng, dims, split, smallest, top_value):
    factor_of, own = 1.0, jax.random.fold_in(rng, 6)
    for dim, shards_of in split:
        draws = jnp.exp(jax.random.uniform(jax.random.fold_in(own, dim), (shards_of,), jnp.float32, smallest / len(split), top_value / len(split)))
        factor_of = factor_of * jnp.repeat(draws, dims[dim] // shards_of).reshape([-1 if axis == dim else 1 for axis in range(len(dims))])
    return factor_of


def bell_draw(stream_key, dims, width, limit, shards=(), held_as=jnp.bfloat16):
    array = jax.random.normal(stream_key, dims, jnp.float32) * width
    if len(shards) > 0:
        array = levels(stream_key, dims, shards, -0.22, 0.18) * array
    return jnp.clip(array, min=-limit, max=limit).astype(held_as)


def setup_inputs(seed: int = 0) -> dict:
    key_of = jax.random.split(jax.random.key(seed), 9)
    return {
        "queries": draw_queries(jax.random.fold_in(key_of[8], 71), 0),
        "cached_keys": draw_cached_keys(jax.random.fold_in(key_of[8], 71), 0),
        "values": bell_draw(key_of[2], (TOKENS, KVH * HEAD_DIM), 1.0, 6.0, ((0, 8), (1, 4))),
        "patch_keys": bell_draw(key_of[3], (TOKENS, KVH * HEAD_DIM), 1.0, 6.0, ((0, 8), (1, 4))),
        "out_grad": bell_draw(key_of[4], (TOKENS, MODEL), 1.0, 6.0, ((0, 8), (1, 4))),
        "out_weight": bell_draw(key_of[5], (QH * HEAD_DIM, MODEL), (QH * HEAD_DIM) ** -0.5, 0.09375, ((0, 4),)),
        "knocked": touch_ends((jax.random.randint(key_of[6], (KVH,), 0, 2) < 1).astype(jnp.int32), jax.random.fold_in(key_of[6], 1), 0, 1),
        "patch_start": touch_ends(jax.random.randint(key_of[7], (KVH,), 0, TOKENS), jax.random.fold_in(key_of[7], 1), 0, TOKENS - 1).astype(jnp.int32),
    }


LOGIT_SCALE = 168.0 ** -0.5


def patch_select(cached_keys, patch_keys, knocked, patch_start):
    head_size = cached_keys.shape[1] // knocked.shape[0]
    positions = jnp.arange(cached_keys.shape[0], dtype=jnp.int32)
    chosen = (jnp.repeat(knocked, head_size)[None, :] == 1) & (positions[:, None] >= jnp.repeat(patch_start, head_size)[None, :])
    return chosen, jnp.where(chosen, patch_keys, cached_keys)


def reference(queries, cached_keys, values, patch_keys, out_grad, out_weight, knocked, patch_start):
    chosen, patched = patch_select(cached_keys, patch_keys, knocked, patch_start)
    out_grads = jnp.dot(out_grad, out_weight.T, preferred_element_type=jnp.float32).astype(jnp.bfloat16)
    key_width = patched.shape[1]
    padding = jnp.zeros((WINDOW, key_width), jnp.bfloat16)
    keys_padded = jnp.concatenate([padding, patched], axis=0)
    values_padded = jnp.concatenate([padding, values], axis=0)
    key_span = WINDOW + TOK_DEV
    row_ids = jnp.arange(TOK_DEV, dtype=jnp.int32)[:, None]
    col_ids = jnp.arange(key_span, dtype=jnp.int32)[None, :]
    band = (col_ids > row_ids) & (col_ids <= row_ids + WINDOW)

    def one_block(totals, block_index):
        row_start = block_index * TOK_DEV
        allowed = band & (col_ids + row_start >= WINDOW)
        query_tile = lax.dynamic_slice_in_dim(queries, row_start, TOK_DEV, 0).astype(jnp.float32).reshape(TOK_DEV, KVH, 2, HEAD_DIM)
        key_tile = lax.dynamic_slice_in_dim(keys_padded, row_start, key_span, 0).astype(jnp.float32).reshape(key_span, KVH, HEAD_DIM)
        value_tile = lax.dynamic_slice_in_dim(values_padded, row_start, key_span, 0).astype(jnp.float32).reshape(key_span, KVH, HEAD_DIM)
        gradient_block = lax.dynamic_slice_in_dim(out_grads, row_start, TOK_DEV, 0).astype(jnp.float32).reshape(TOK_DEV, KVH, 2, HEAD_DIM)
        logit_scores = jnp.einsum("xwob,nwb->woxn", query_tile, key_tile) * LOGIT_SCALE
        logit_scores = jnp.where(allowed, logit_scores, -jnp.inf)
        maxima = jnp.max(logit_scores, axis=-1, keepdims=True)
        raised = jnp.exp(logit_scores - maxima)
        attention = raised / jnp.sum(raised, axis=-1, keepdims=True)
        attention_reduced = lax.optimization_barrier(attention.astype(jnp.bfloat16)).astype(jnp.float32)
        attended_rows = jnp.einsum("eyzf,feq->zeyq", attention_reduced, value_tile).astype(jnp.bfloat16)
        gradient_scores = jnp.einsum("xwob,nwb->woxn", gradient_block, value_tile)
        centre = jnp.sum(attention * gradient_scores, axis=-1, keepdims=True)
        score_gradient = lax.optimization_barrier((attention * (gradient_scores - centre)).astype(jnp.bfloat16)).astype(jnp.float32)
        query_gradient = (LOGIT_SCALE * jnp.einsum("eyzf,feq->zeyq", score_gradient, key_tile)).astype(jnp.bfloat16)
        key_portion = LOGIT_SCALE * jnp.einsum("mjhq,hmju->qmu", score_gradient, query_tile)
        value_portion = jnp.einsum("mjhq,hmju->qmu", attention_reduced, gradient_block)
        key_total, value_total = totals
        key_total = lax.dynamic_update_slice_in_dim(key_total, lax.dynamic_slice_in_dim(key_total, row_start, key_span, 0) + key_portion.reshape(key_span, key_width), row_start, 0)
        value_total = lax.dynamic_update_slice_in_dim(value_total, lax.dynamic_slice_in_dim(value_total, row_start, key_span, 0) + value_portion.reshape(key_span, key_width), row_start, 0)
        return (key_total, value_total), (query_gradient.reshape(TOK_DEV, -1), attended_rows.reshape(TOK_DEV, -1))

    start_totals = (jnp.zeros((WINDOW + TOKENS, key_width), jnp.float32), jnp.zeros((WINDOW + TOKENS, key_width), jnp.float32))
    (key_total, value_total), (query_all, attended_all) = lax.scan(one_block, start_totals, jnp.arange(TOKENS // TOK_DEV, dtype=jnp.int32))
    query_grad = query_all.reshape(TOKENS, -1)
    attended_all = attended_all.reshape(TOKENS, -1)
    key_sums = key_total[WINDOW:]
    key_grad = jnp.where(chosen, jnp.float32(0.0), key_sums).astype(jnp.bfloat16)
    patch_grad = jnp.where(chosen, key_sums, jnp.float32(0.0)).astype(jnp.bfloat16)
    value_grad = value_total[WINDOW:].astype(jnp.bfloat16)
    weight_grad = jnp.dot(attended_all.T, out_grad, preferred_element_type=jnp.float32)
    return query_grad, key_grad, value_grad, patch_grad, weight_grad
```

```python
import functools

import jax
import jax.numpy as jnp
from jax import lax
from jax.experimental import pallas as pl
from jax.experimental.pallas import tpu as pltpu
from jax.sharding import PartitionSpec as P

LOGIT_SCALE = 168.0 ** (-0.5)
EXP2_SCALE = LOGIT_SCALE * 1.4426950408889634
TILE = 256
VMEM_LIMIT = 48 * 1024 * 1024
CHEAP = pl.CostEstimate(flops=1, bytes_accessed=1, transcendentals=0)

NT = (((1,), (1,)), ((), ()))
NN = (((1,), (0,)), ((), ()))


def dot(a, b, dims=NN):
    return lax.dot_general(a, b, dims, preferred_element_type=jnp.float32)


def stack_heads(pair, head_size):
    return jnp.concatenate([pair[:, :head_size], pair[:, head_size:]], axis=0)


def forward_kernel(chip_ref, q_ref, k_ref, v_ref, pk_ref, pv_ref, p_ref, at_ref, keys, values_t):
    tile = pl.program_id(1)
    rows, head_size = k_ref.shape
    blocks = rows // TILE

    @pl.when(tile == 0)
    def _():
        keys[:rows] = pk_ref[...]
        keys[rows:] = k_ref[...]
        values_t[:, :rows] = pv_ref[...].T
        values_t[:, rows:] = v_ref[...].T

    q = stack_heads(q_ref[...], head_size)
    key_id = lax.broadcasted_iota(jnp.int32, (TILE, 2 * TILE), 0)
    query_id = lax.broadcasted_iota(jnp.int32, (TILE, 2 * TILE), 1) & (TILE - 1)
    first = chip_ref[0] == 0
    top = None
    for b in range(blocks + 1):
        start = pl.multiple_of((tile + b) * TILE, TILE)
        s = dot(keys[pl.ds(start, TILE), :], q, NT)
        if b == 0:
            s = jnp.where(key_id > query_id, s, -jnp.inf)
        if b == blocks:
            s = jnp.where(key_id <= query_id, s, -jnp.inf)
        else:
            s = s + jnp.where(jnp.logical_and(first, tile + b < blocks), -jnp.inf, 0.0)
        p_ref[0, 0, b * TILE : (b + 1) * TILE, :] = s
        here = jnp.max(s, axis=0, keepdims=True)
        top = here if top is None else jnp.maximum(top, here)
    total = None
    for b in range(blocks + 1):
        part = pl.ds(b * TILE, TILE)
        e = jnp.exp2((p_ref[0, 0, part, :] - top) * EXP2_SCALE)
        p_ref[0, 0, part, :] = e
        here = jnp.sum(e, axis=0, keepdims=True)
        total = here if total is None else total + here
    inverse = 1.0 / total
    out = None
    for b in range(blocks + 1):
        part = pl.ds(b * TILE, TILE)
        start = pl.multiple_of((tile + b) * TILE, TILE)
        p = p_ref[0, 0, part, :] * inverse
        p_ref[0, 0, part, :] = p
        term = dot(values_t[:, pl.ds(start, TILE)], p.astype(jnp.bfloat16))
        out = term if out is None else out + term
    at_ref[:head_size] = out[:, :TILE].astype(jnp.bfloat16)
    at_ref[head_size:] = out[:, TILE:].astype(jnp.bfloat16)


def forward(chip, packet, before, head_size):
    rows = packet.shape[0]
    groups = packet.shape[1] // (4 * head_size)
    tiles = rows // TILE
    span = rows + TILE
    grid_spec = pltpu.PrefetchScalarGridSpec(
        num_scalar_prefetch=1,
        grid=(groups, tiles),
        in_specs=[
            pl.BlockSpec((TILE, 2 * head_size), lambda g, i, c: (i, g)),
            pl.BlockSpec((rows, head_size), lambda g, i, c: (0, 2 * groups + g)),
            pl.BlockSpec((rows, head_size), lambda g, i, c: (0, 3 * groups + g)),
            pl.BlockSpec((rows, head_size), lambda g, i, c: (0, g)),
            pl.BlockSpec((rows, head_size), lambda g, i, c: (0, groups + g)),
        ],
        out_specs=[
            pl.BlockSpec((1, 1, span, 2 * TILE), lambda g, i, c: (g, i, 0, 0)),
            pl.BlockSpec((2 * head_size, TILE), lambda g, i, c: (g, i)),
        ],
        scratch_shapes=[
            pltpu.VMEM((2 * rows, head_size), jnp.bfloat16),
            pltpu.VMEM((head_size, 2 * rows), jnp.bfloat16),
        ],
    )
    return pl.pallas_call(
        forward_kernel,
        grid_spec=grid_spec,
        out_shape=[
            jax.ShapeDtypeStruct((groups, tiles, span, 2 * TILE), jnp.float32),
            jax.ShapeDtypeStruct((groups * 2 * head_size, rows), jnp.bfloat16),
        ],
        compiler_params=pltpu.CompilerParams(vmem_limit_bytes=VMEM_LIMIT),
        cost_estimate=CHEAP,
        name="attention_forward",
    )(chip, packet, packet, packet, before, before)


def backward_kernel(
    phase, q_ref, k_ref, v_ref, pk_ref, pv_ref, p_ref, do_ref, carry_ref, dq_ref, dprev_ref, keep_ref, keys_t, values, dk, dv, dp
):
    tile = pl.program_id(1)
    rows, head_size = k_ref.shape
    blocks = rows // TILE
    half = rows // 2
    old = rows - phase * half

    @pl.when(tile == 0)
    def _():
        keys_t[:, :old] = pk_ref[rows - old :, :].T
        keys_t[:, old:] = k_ref[: half + rows - old, :].T
        values[:old] = pv_ref[rows - old :, :]
        values[old:] = v_ref[: half + rows - old, :]
        if phase == 0:
            dk[...] = jnp.zeros_like(dk)
            dv[...] = jnp.zeros_like(dv)
        else:
            dk[:rows] = carry_ref[0, 0]
            dv[:rows] = carry_ref[1, 0]
            dk[rows:] = jnp.zeros((half, head_size), jnp.float32)
            dv[rows:] = jnp.zeros((half, head_size), jnp.float32)

    q = stack_heads(q_ref[...], head_size)
    do = jnp.concatenate([do_ref[:head_size], do_ref[head_size:]], axis=1)
    centre = None
    for b in range(blocks + 1):
        start = pl.multiple_of((tile + b) * TILE, TILE)
        part = pl.ds(b * TILE, TILE)
        p = p_ref[0, 0, part, :]
        grad = dot(values[pl.ds(start, TILE), :], do)
        dp[part, :] = grad
        here = jnp.sum(p * grad, axis=0, keepdims=True)
        centre = here if centre is None else centre + here
        dv[pl.ds(start, TILE), :] += dot(p.astype(jnp.bfloat16), do, NT)
    out = None
    for b in range(blocks + 1):
        start = pl.multiple_of((tile + b) * TILE, TILE)
        part = pl.ds(b * TILE, TILE)
        ds = (p_ref[0, 0, part, :] * (dp[part, :] - centre)).astype(jnp.bfloat16)
        dk[pl.ds(start, TILE), :] += dot(ds, q)
        term = dot(keys_t[:, pl.ds(start, TILE)], ds)
        out = term if out is None else out + term
    out = out * LOGIT_SCALE
    dq_ref[:, :head_size] = out[:, :TILE].T.astype(jnp.bfloat16)
    dq_ref[:, head_size:] = out[:, TILE:].T.astype(jnp.bfloat16)

    @pl.when(tile == pl.num_programs(1) - 1)
    def _():
        dprev_ref[0, 0] = (dk[:half] * LOGIT_SCALE).astype(jnp.bfloat16)
        dprev_ref[1, 0] = dv[:half].astype(jnp.bfloat16)
        keep_ref[0, 0] = dk[half:]
        keep_ref[1, 0] = dv[half:]


def backward(phase, members, packet, before, attention, out_grads, carry, head_size):
    rows = packet.shape[0]
    groups = packet.shape[1] // (4 * head_size)
    g0, count = members
    tiles = rows // TILE // 2
    half = rows // 2
    span = rows + TILE
    first = phase * tiles
    if carry is None:
        carry = jnp.zeros((2, 1, 8, head_size), jnp.float32)
        carry_spec = pl.BlockSpec((2, 1, 8, head_size), lambda g, i: (0, 0, 0, 0))
    else:
        carry_spec = pl.BlockSpec((2, 1, rows, head_size), lambda g, i: (0, g0 + g, 0, 0))
    return pl.pallas_call(
        functools.partial(backward_kernel, phase),
        grid=(count, tiles),
        in_specs=[
            pl.BlockSpec((TILE, 2 * head_size), lambda g, i: (first + i, g0 + g)),
            pl.BlockSpec((rows, head_size), lambda g, i: (0, 2 * groups + g0 + g)),
            pl.BlockSpec((rows, head_size), lambda g, i: (0, 3 * groups + g0 + g)),
            pl.BlockSpec((rows, head_size), lambda g, i: (0, g0 + g)),
            pl.BlockSpec((rows, head_size), lambda g, i: (0, groups + g0 + g)),
            pl.BlockSpec((1, 1, span, 2 * TILE), lambda g, i: (g0 + g, first + i, 0, 0)),
            pl.BlockSpec((2 * head_size, TILE), lambda g, i: (g0 + g, i)),
            carry_spec,
        ],
        out_specs=[
            pl.BlockSpec((TILE, 2 * head_size), lambda g, i: (i, g)),
            pl.BlockSpec((2, 1, half, head_size), lambda g, i: (0, g, 0, 0)),
            pl.BlockSpec((2, 1, rows, head_size), lambda g, i: (0, g, 0, 0)),
        ],
        out_shape=[
            jax.ShapeDtypeStruct((half, count * 2 * head_size), jnp.bfloat16),
            jax.ShapeDtypeStruct((2, count, half, head_size), jnp.bfloat16),
            jax.ShapeDtypeStruct((2, count, rows, head_size), jnp.float32),
        ],
        scratch_shapes=[
            pltpu.VMEM((head_size, rows + half), jnp.bfloat16),
            pltpu.VMEM((rows + half, head_size), jnp.bfloat16),
            pltpu.VMEM((rows + half, head_size), jnp.float32),
            pltpu.VMEM((rows + half, head_size), jnp.float32),
            pltpu.VMEM((span, 2 * TILE), jnp.float32),
        ],
        compiler_params=pltpu.CompilerParams(vmem_limit_bytes=VMEM_LIMIT),
        cost_estimate=CHEAP,
        name="attention_backward",
    )(packet, packet, packet, before, before, attention, out_grads, carry)


def grads_kernel(block_ref, weight_ref, *refs):
    total = dot(weight_ref[...], block_ref[0])
    if len(refs) == 2:
        total = total + refs[0][...]
    refs[-1][...] = total.astype(refs[-1].dtype)


def add_grads(block, weight, total, at, dtype):
    parts, cols, tok = block.shape
    width = weight.shape[0]
    tiles = tok // TILE
    return pl.pallas_call(
        grads_kernel,
        grid=(parts * tiles,),
        in_specs=[
            pl.BlockSpec((1, cols, TILE), lambda i: (i // tiles, 0, i % tiles)),
            pl.BlockSpec((width, cols), lambda i: (0, 0)),
        ]
        + ([] if total is None else [pl.BlockSpec((width, TILE), lambda i: (0, at // TILE + i))]),
        out_specs=pl.BlockSpec((width, TILE), lambda i: (0, i)),
        out_shape=jax.ShapeDtypeStruct((width, parts * tok), dtype),
        compiler_params=pltpu.CompilerParams(vmem_limit_bytes=VMEM_LIMIT),
        name="out_grads",
    )(block, weight, *([] if total is None else [total]))


def terms_kernel(count, rows_ref, *refs):
    blocks, outs = refs[: len(refs) - count], refs[len(refs) - count :]
    share = rows_ref.shape[0] // count
    term, at = None, 0
    for block in blocks:
        for part in range(block.shape[0]):
            width = block.shape[2]
            piece = dot(rows_ref[:, at : at + width], block[part], NT)
            term = piece if term is None else term + piece
            at += width
    for s in range(count):
        outs[s][...] = term[s * share : (s + 1) * share].astype(outs[s].dtype)


def make_terms(rows, blocks, count, chunk):
    cols = blocks[0].shape[1]
    share = rows.shape[0] // count
    return pl.pallas_call(
        functools.partial(terms_kernel, count),
        grid=(cols // chunk,),
        in_specs=[pl.BlockSpec(rows.shape, lambda i: (0, 0))]
        + [pl.BlockSpec((block.shape[0], chunk, block.shape[2]), lambda i: (0, i, 0)) for block in blocks],
        out_specs=[pl.BlockSpec((share, chunk), lambda i: (0, i))] * count,
        out_shape=[jax.ShapeDtypeStruct((share, cols), jnp.float32 if s == 0 else jnp.bfloat16) for s in range(count)],
        compiler_params=pltpu.CompilerParams(vmem_limit_bytes=VMEM_LIMIT),
        name="weight_terms",
    )(rows, *blocks)


def shift(shard, by):
    size = lax.axis_size("ctx")
    return lax.ppermute(shard, "ctx", [(i, i + by) for i in range(size) if 0 <= i + by < size])


def swap_cores(shard, only=None):
    size = lax.axis_size("ctx")
    return lax.ppermute(shard, "ctx", [(i, i ^ 1) for i in range(size) if only is None or i % 2 == only])


def gather_chip(block):
    n_ctx, n_head = lax.axis_size("ctx"), lax.axis_size("head")
    groups = [[c * n_head + i for i in range(2 * n_head)] for c in range(0, n_ctx, 2)]
    whole = lax.all_gather(block, ("ctx", "head"), axis=0, axis_index_groups=groups)
    return whole.reshape(2, n_head * block.shape[0], block.shape[1])


def after(values, *others):
    return lax.optimization_barrier((values, *others))[0]


def body(queries, cached_keys, values, patch_keys, out_grad, out_weight, knocked, patch_start):
    tok = queries.shape[0]
    kv_local = knocked.shape[0]
    head_size = cached_keys.shape[1] // kv_local
    cols = out_grad.shape[1]
    out_grad = out_grad.T
    n_head, n_ctx = lax.axis_size("head"), lax.axis_size("ctx")
    chips = n_ctx // 2
    place, z = lax.axis_index("ctx"), lax.axis_index("head")
    core, chip = place % 2, place // 2
    low = core == 0
    half_q, half_kv = queries.shape[1] // 2, cached_keys.shape[1] // 2
    dyn = lax.dynamic_slice_in_dim

    positions = place * tok + jnp.arange(tok, dtype=jnp.int32)
    chosen = (jnp.repeat(knocked, head_size)[None, :] == 1) & (
        positions[:, None] >= jnp.repeat(patch_start, head_size)[None, :]
    )
    patched = jnp.where(chosen, patch_keys, cached_keys)

    def packet_of(which):
        return jnp.concatenate(
            [
                dyn(queries, which * half_q, half_q, 1),
                dyn(patched, which * half_kv, half_kv, 1),
                dyn(values, which * half_kv, half_kv, 1),
            ],
            axis=1,
        )

    mine, other = packet_of(core), swap_cores(packet_of(1 - core))
    packet = jnp.concatenate([jnp.where(low, mine, other), jnp.where(low, other, mine)], axis=0)
    before = shift(packet[:, half_q:], 2)

    cut = 2 * cols // 3
    quarter = tok // 2
    first = gather_chip(out_grad[:cut])
    rest = out_grad[cut:]
    passed = swap_cores(jnp.where(low, rest[:, quarter:], rest[:, :quarter]))
    second = gather_chip(jnp.where(low, rest[:, :quarter], passed))
    third = gather_chip(jnp.where(low, passed, rest[:, quarter:]))

    weight_half = dyn(out_weight, core * half_q, half_q, 0).reshape(half_q, n_head, cols)
    first_weight = weight_half[:, :, :cut].reshape(half_q, n_head * cut)
    rest_weight = weight_half[:, :, cut:].reshape(half_q, n_head * (cols - cut))
    before = after(before, first_weight, rest_weight)

    attention, attended = forward(chip[None].astype(jnp.int32), packet, before, head_size)
    share = out_weight.shape[0] // n_ctx
    parity = attended.reshape(chips // 2, 2, share, 2 * tok)
    kept, given = dyn(parity, core, 1, 1)[:, 0], dyn(parity, 1 - core, 1, 1)[:, 0]
    taken = swap_cores(given)
    by_chip = jnp.concatenate([jnp.where(low, kept, taken), jnp.where(low, taken, kept)], axis=0)
    by_distance = jnp.concatenate([dyn(by_chip, chip ^ s, 1, 0) for s in range(chips)], axis=0)
    by_distance = by_distance.reshape(chips * share, 2 * tok)

    def send_terms(blocks, chunk):
        kept_term, *sent = make_terms(by_distance, blocks, chips, chunk)
        got = [lax.ppermute(x, "ctx", [(i, i ^ (2 * s + 2)) for i in range(n_ctx)]) for s, x in enumerate(sent)]
        return kept_term, sent, got

    first_terms = send_terms([first], 2 * TILE)
    grads = add_grads(first, first_weight, None, 0, jnp.float32)
    grads, _ = lax.optimization_barrier((grads, first_terms[1]))
    all_groups = (0, packet.shape[1] // (4 * head_size))
    grads_low = add_grads(second, rest_weight, grads, 0, jnp.bfloat16)
    query_low, prev_low, carry = backward(0, all_groups, packet, before, attention, grads_low, None, head_size)
    from_low = shift(prev_low, -2)

    third, query_low, first_terms = lax.optimization_barrier((third, query_low, first_terms))
    last_terms = send_terms([second, third], TILE)
    grads_high = add_grads(third, rest_weight, grads, tok, jnp.bfloat16)
    grads_high = after(grads_high, last_terms[1])
    parts = []
    for g in range(all_groups[1]):
        if g == all_groups[1] - 1:
            grads_high, from_low = lax.optimization_barrier((grads_high, from_low))
        parts.append(backward(1, (g, 1), packet, before, attention, grads_high, carry, head_size))
    from_high = jnp.concatenate([shift(part[1], -2) for part in parts], axis=1)
    query_high = jnp.concatenate([part[0] for part in parts], axis=1)
    own = jnp.concatenate([part[2] for part in parts], axis=1)

    sums = [functools.reduce(jnp.add, t[2], t[0]).reshape(share, n_head, -1) for t in (first_terms, last_terms)]
    weight_grad = jnp.concatenate(sums, axis=2).reshape(share, -1)

    query_kept = jnp.where(low, query_low, query_high)
    query_taken = jnp.where(low, swap_cores(query_low, 1), swap_cores(query_high, 0))
    query_grad = jnp.concatenate(
        [jnp.where(low, query_kept, query_taken), jnp.where(low, query_taken, query_kept)], axis=1
    )

    scale = jnp.array([LOGIT_SCALE, 1.0], jnp.float32)[:, None, None, None]
    sums_low = scale * own[:, :, :tok] + from_low
    sums_high = scale * own[:, :, tok:] + from_high
    sums_kept = jnp.where(low, sums_low, sums_high)
    sums_taken = swap_cores(jnp.where(low, sums_high, sums_low).astype(jnp.bfloat16)).astype(jnp.float32)
    sums = jnp.concatenate(
        [jnp.where(low, sums_kept, sums_taken), jnp.where(low, sums_taken, sums_kept)], axis=1
    )
    key_sums, value_sums = [jnp.concatenate([part[h] for h in range(kv_local)], axis=1) for part in (sums[0], sums[1])]
    key_grad = jnp.where(chosen, jnp.float32(0.0), key_sums).astype(jnp.bfloat16)
    patch_grad = jnp.where(chosen, key_sums, jnp.float32(0.0)).astype(jnp.bfloat16)
    value_grad = value_sums.astype(jnp.bfloat16)
    return (query_grad, key_grad, value_grad, patch_grad, weight_grad)


def solution(mesh):
    split = P("ctx", "head")
    return jax.shard_map(
        body,
        mesh=mesh,
        in_specs=(split, split, split, split, split, P("head", None), P("head"), P("head")),
        out_specs=(split, split, split, split, P(("head", "ctx"), None)),
        check_vma=False,
    )
```

```python
import functools

import jax
import jax.numpy as jnp
from jax import lax
from jax.experimental import pallas as pl
from jax.experimental.pallas import tpu as pltpu
from jax.sharding import PartitionSpec as P

LOGIT_SCALE = 168.0 ** (-0.5)
EXP2_SCALE = LOGIT_SCALE * 1.4426950408889634
TILE = 256
VMEM_LIMIT = 24 * 1024 * 1024
ATTENTION_VMEM_LIMIT = 48 * 1024 * 1024
CHEAP = pl.CostEstimate(flops=1, bytes_accessed=1, transcendentals=0)

NT = (((1,), (1,)), ((), ()))
NN = (((1,), (0,)), ((), ()))


def dot(a, b, dims=NN):
    return lax.dot_general(a, b, dims, preferred_element_type=jnp.float32)


def stack_heads(pair, head_size):
    return jnp.concatenate([pair[:, :head_size], pair[:, head_size:]], axis=0)


def forward_kernel(chip_ref, q_ref, k_ref, v_ref, pk_ref, pv_ref, p_ref, at_ref, keys, values_t):
    tile = pl.program_id(1)
    rows, head_size = k_ref.shape
    blocks = rows // TILE

    @pl.when(tile == 0)
    def _():
        keys[:rows] = pk_ref[...]
        keys[rows:] = k_ref[...]
        values_t[:, :rows] = pv_ref[...].T
        values_t[:, rows:] = v_ref[...].T

    q = stack_heads(q_ref[...], head_size)
    key_id = lax.broadcasted_iota(jnp.int32, (TILE, 2 * TILE), 0)
    query_id = lax.broadcasted_iota(jnp.int32, (TILE, 2 * TILE), 1) & (TILE - 1)
    first = chip_ref[0] == 0
    top = None
    for b in range(blocks + 1):
        start = pl.multiple_of((tile + b) * TILE, TILE)
        s = dot(keys[pl.ds(start, TILE), :], q, NT)
        if b == 0:
            s = jnp.where(key_id > query_id, s, -jnp.inf)
        if b == blocks:
            s = jnp.where(key_id <= query_id, s, -jnp.inf)
        else:
            s = s + jnp.where(jnp.logical_and(first, tile + b < blocks), -jnp.inf, 0.0)
        p_ref[0, 0, b * TILE : (b + 1) * TILE, :] = s
        here = jnp.max(s, axis=0, keepdims=True)
        top = here if top is None else jnp.maximum(top, here)
    total = None
    for b in range(blocks + 1):
        part = pl.ds(b * TILE, TILE)
        e = jnp.exp2((p_ref[0, 0, part, :] - top) * EXP2_SCALE)
        p_ref[0, 0, part, :] = e
        here = jnp.sum(e, axis=0, keepdims=True)
        total = here if total is None else total + here
    inverse = 1.0 / total
    out = None
    for b in range(blocks + 1):
        part = pl.ds(b * TILE, TILE)
        start = pl.multiple_of((tile + b) * TILE, TILE)
        p = p_ref[0, 0, part, :] * inverse
        p_ref[0, 0, part, :] = p
        term = dot(values_t[:, pl.ds(start, TILE)], p.astype(jnp.bfloat16))
        out = term if out is None else out + term
    at_ref[:head_size] = out[:, :TILE].astype(jnp.bfloat16)
    at_ref[head_size:] = out[:, TILE:].astype(jnp.bfloat16)


def forward(chip, packet, before, head_size):
    rows = packet.shape[0]
    groups = packet.shape[1] // (4 * head_size)
    tiles = rows // TILE
    span = rows + TILE
    grid_spec = pltpu.PrefetchScalarGridSpec(
        num_scalar_prefetch=1,
        grid=(groups, tiles),
        in_specs=[
            pl.BlockSpec((TILE, 2 * head_size), lambda g, i, c: (i, g)),
            pl.BlockSpec((rows, head_size), lambda g, i, c: (0, 2 * groups + g)),
            pl.BlockSpec((rows, head_size), lambda g, i, c: (0, 3 * groups + g)),
            pl.BlockSpec((rows, head_size), lambda g, i, c: (0, g)),
            pl.BlockSpec((rows, head_size), lambda g, i, c: (0, groups + g)),
        ],
        out_specs=[
            pl.BlockSpec((1, 1, span, 2 * TILE), lambda g, i, c: (g, i, 0, 0)),
            pl.BlockSpec((2 * head_size, TILE), lambda g, i, c: (g, i)),
        ],
        scratch_shapes=[
            pltpu.VMEM((2 * rows, head_size), jnp.bfloat16),
            pltpu.VMEM((head_size, 2 * rows), jnp.bfloat16),
        ],
    )
    return pl.pallas_call(
        forward_kernel,
        grid_spec=grid_spec,
        out_shape=[
            jax.ShapeDtypeStruct((groups, tiles, span, 2 * TILE), jnp.float32),
            jax.ShapeDtypeStruct((groups * 2 * head_size, rows), jnp.bfloat16),
        ],
        compiler_params=pltpu.CompilerParams(vmem_limit_bytes=ATTENTION_VMEM_LIMIT),
        cost_estimate=CHEAP,
        name="attention_forward",
    )(chip, packet, packet, packet, before, before)


def backward_kernel(
    phase, q_ref, k_ref, v_ref, pk_ref, pv_ref, p_ref, do_ref, carry_ref, dq_ref, dprev_ref, keep_ref, keys_t, values, dk, dv, dp
):
    tile = pl.program_id(1)
    rows, head_size = k_ref.shape
    blocks = rows // TILE
    half = rows // 2
    old = rows - phase * half

    @pl.when(tile == 0)
    def _():
        keys_t[:, :old] = pk_ref[rows - old :, :].T
        keys_t[:, old:] = k_ref[: half + rows - old, :].T
        values[:old] = pv_ref[rows - old :, :]
        values[old:] = v_ref[: half + rows - old, :]
        if phase == 0:
            dk[...] = jnp.zeros_like(dk)
            dv[...] = jnp.zeros_like(dv)
        else:
            dk[:rows] = carry_ref[0, 0]
            dv[:rows] = carry_ref[1, 0]
            dk[rows:] = jnp.zeros((half, head_size), jnp.float32)
            dv[rows:] = jnp.zeros((half, head_size), jnp.float32)

    q = stack_heads(q_ref[...], head_size)
    do = jnp.concatenate([do_ref[:head_size], do_ref[head_size:]], axis=1)
    centre = None
    for b in range(blocks + 1):
        start = pl.multiple_of((tile + b) * TILE, TILE)
        part = pl.ds(b * TILE, TILE)
        p = p_ref[0, 0, part, :]
        grad = dot(values[pl.ds(start, TILE), :], do)
        dp[part, :] = grad
        here = jnp.sum(p * grad, axis=0, keepdims=True)
        centre = here if centre is None else centre + here
        dv[pl.ds(start, TILE), :] += dot(p.astype(jnp.bfloat16), do, NT)
    out = None
    for b in range(blocks + 1):
        start = pl.multiple_of((tile + b) * TILE, TILE)
        part = pl.ds(b * TILE, TILE)
        ds = (p_ref[0, 0, part, :] * (dp[part, :] - centre)).astype(jnp.bfloat16)
        dk[pl.ds(start, TILE), :] += dot(ds, q)
        term = dot(keys_t[:, pl.ds(start, TILE)], ds)
        out = term if out is None else out + term
    out = out * LOGIT_SCALE
    dq_ref[:, :head_size] = out[:, :TILE].T.astype(jnp.bfloat16)
    dq_ref[:, head_size:] = out[:, TILE:].T.astype(jnp.bfloat16)

    @pl.when(tile == pl.num_programs(1) - 1)
    def _():
        dprev_ref[0, 0] = (dk[:half] * LOGIT_SCALE).astype(jnp.bfloat16)
        dprev_ref[1, 0] = dv[:half].astype(jnp.bfloat16)
        keep_ref[0, 0] = dk[half:]
        keep_ref[1, 0] = dv[half:]


def backward(phase, members, packet, before, attention, out_grads, carry, head_size):
    rows = packet.shape[0]
    groups = packet.shape[1] // (4 * head_size)
    g0, count = members
    tiles = rows // TILE // 2
    half = rows // 2
    span = rows + TILE
    first = phase * tiles
    if carry is None:
        carry = jnp.zeros((2, 1, 8, head_size), jnp.float32)
        carry_spec = pl.BlockSpec((2, 1, 8, head_size), lambda g, i: (0, 0, 0, 0))
    else:
        carry_spec = pl.BlockSpec((2, 1, rows, head_size), lambda g, i: (0, g0 + g, 0, 0))
    return pl.pallas_call(
        functools.partial(backward_kernel, phase),
        grid=(count, tiles),
        in_specs=[
            pl.BlockSpec((TILE, 2 * head_size), lambda g, i: (first + i, g0 + g)),
            pl.BlockSpec((rows, head_size), lambda g, i: (0, 2 * groups + g0 + g)),
            pl.BlockSpec((rows, head_size), lambda g, i: (0, 3 * groups + g0 + g)),
            pl.BlockSpec((rows, head_size), lambda g, i: (0, g0 + g)),
            pl.BlockSpec((rows, head_size), lambda g, i: (0, groups + g0 + g)),
            pl.BlockSpec((1, 1, span, 2 * TILE), lambda g, i: (g0 + g, first + i, 0, 0)),
            pl.BlockSpec((2 * head_size, TILE), lambda g, i: (g0 + g, first + i)),
            carry_spec,
        ],
        out_specs=[
            pl.BlockSpec((TILE, 2 * head_size), lambda g, i: (i, g)),
            pl.BlockSpec((2, 1, half, head_size), lambda g, i: (0, g, 0, 0)),
            pl.BlockSpec((2, 1, rows, head_size), lambda g, i: (0, g, 0, 0)),
        ],
        out_shape=[
            jax.ShapeDtypeStruct((half, count * 2 * head_size), jnp.bfloat16),
            jax.ShapeDtypeStruct((2, count, half, head_size), jnp.bfloat16),
            jax.ShapeDtypeStruct((2, count, rows, head_size), jnp.float32),
        ],
        scratch_shapes=[
            pltpu.VMEM((head_size, rows + half), jnp.bfloat16),
            pltpu.VMEM((rows + half, head_size), jnp.bfloat16),
            pltpu.VMEM((rows + half, head_size), jnp.float32),
            pltpu.VMEM((rows + half, head_size), jnp.float32),
            pltpu.VMEM((span, 2 * TILE), jnp.float32),
        ],
        compiler_params=pltpu.CompilerParams(vmem_limit_bytes=ATTENTION_VMEM_LIMIT),
        cost_estimate=CHEAP,
        name="attention_backward",
    )(packet, packet, packet, before, before, attention, out_grads, carry)


def grads_kernel(number, *refs):
    blocks, weights = refs[:number], refs[number : 2 * number]
    total = None
    for block, weight in zip(blocks, weights):
        term = dot(weight[...], block[0])
        total = term if total is None else total + term
    for old in refs[2 * number : -1]:
        total = total + old[...]
    refs[-1][...] = total.astype(refs[-1].dtype)


def add_grads(blocks, weights, total, dtype):
    _, cols, tok = blocks[0].shape
    width = weights[0].shape[0]
    tiles = tok // TILE
    tile_spec = pl.BlockSpec((width, TILE), lambda i: (0, i))
    number = len(blocks)
    return pl.pallas_call(
        functools.partial(grads_kernel, number),
        grid=(2 * tiles,),
        in_specs=[pl.BlockSpec((1, cols, TILE), lambda i: (i // tiles, 0, i % tiles))] * number
        + [pl.BlockSpec((width, cols), lambda i: (0, 0))] * number
        + ([] if total is None else [tile_spec]),
        out_specs=tile_spec,
        out_shape=jax.ShapeDtypeStruct((width, 2 * tok), dtype),
        compiler_params=pltpu.CompilerParams(vmem_limit_bytes=VMEM_LIMIT),
        cost_estimate=CHEAP,
        name="out_grads",
    )(*blocks, *weights, *([] if total is None else [total]))


def terms_kernel(count, rows_ref, block, *outs):
    _, cols, tok = block.shape
    share = rows_ref.shape[0] // count
    for at in range(0, cols, TILE):
        here = slice(at, min(at + TILE, cols))
        term = dot(rows_ref[:, :tok], block[0, here, :], NT) + dot(rows_ref[:, tok:], block[1, here, :], NT)
        for s in range(count):
            outs[s][:, here] = term[s * share : (s + 1) * share].astype(outs[s].dtype)


def make_terms(rows, block, count):
    cols = block.shape[1]
    share = rows.shape[0] // count
    whole = lambda *shape: pl.BlockSpec(shape, lambda i: (0,) * len(shape))
    shapes = [jax.ShapeDtypeStruct((share, cols), jnp.float32 if s == 0 else jnp.bfloat16) for s in range(count)]
    return pl.pallas_call(
        functools.partial(terms_kernel, count),
        grid=(1,),
        in_specs=[whole(*rows.shape), whole(*block.shape)],
        out_specs=[whole(share, cols)] * count,
        out_shape=shapes,
        compiler_params=pltpu.CompilerParams(vmem_limit_bytes=VMEM_LIMIT),
        cost_estimate=CHEAP,
        name="weight_terms",
    )(rows, block)


def close_kernel(groups, core_ref, from_low_ref, *refs):
    owns, highs, (keep_ref, send_ref) = refs[:groups], refs[groups : 2 * groups], refs[2 * groups :]
    half = from_low_ref.shape[2]

    def write(low_ref, high_ref):
        for part in range(2):
            scale = LOGIT_SCALE if part == 0 else 1.0
            for g in range(groups):
                low = owns[g][part, 0, :half] * scale + from_low_ref[part, g].astype(jnp.float32)
                high = owns[g][part, 0, half:] * scale + highs[g][part, 0].astype(jnp.float32)
                low_ref[part, g] = low.astype(jnp.bfloat16)
                high_ref[part, g] = high.astype(jnp.bfloat16)

    @pl.when(core_ref[0] == 0)
    def _():
        write(keep_ref, send_ref)

    @pl.when(core_ref[0] == 1)
    def _():
        write(send_ref, keep_ref)


def close_sums(core, from_low, owns, highs):
    whole = lambda x: pl.BlockSpec(x.shape, lambda i, c: (0,) * x.ndim)
    out = jax.ShapeDtypeStruct(from_low.shape, jnp.bfloat16)
    return pl.pallas_call(
        functools.partial(close_kernel, len(owns)),
        grid_spec=pltpu.PrefetchScalarGridSpec(
            num_scalar_prefetch=1,
            grid=(1,),
            in_specs=[whole(x) for x in (from_low, *owns, *highs)],
            out_specs=[whole(out), whole(out)],
        ),
        out_shape=[out, out],
        compiler_params=pltpu.CompilerParams(vmem_limit_bytes=VMEM_LIMIT),
        cost_estimate=CHEAP,
        name="close_sums",
    )(core, from_low, *owns, *highs)


def place_kernel(where_ref, knocked_ref, start_ref, keep_ref, taken_ref, key_ref, value_ref, patch_ref):
    groups, tok, head_size = keep_ref.shape[1:]
    core, row_start = where_ref[0], where_ref[1]
    positions = row_start + lax.broadcasted_iota(jnp.int32, (tok, head_size), 0)
    for head in range(2 * groups):
        own = core == head // groups
        at = slice(head * head_size, (head + 1) * head_size)
        both = [
            jnp.where(own, keep_ref[part, head % groups].astype(jnp.float32), taken_ref[part, head % groups].astype(jnp.float32))
            for part in range(2)
        ]
        chosen = jnp.logical_and(knocked_ref[head] == 1, positions >= start_ref[head])
        key_ref[:, at] = jnp.where(chosen, 0.0, both[0]).astype(jnp.bfloat16)
        patch_ref[:, at] = jnp.where(chosen, both[0], 0.0).astype(jnp.bfloat16)
        value_ref[:, at] = both[1].astype(jnp.bfloat16)


def place_sums(where, knocked, patch_start, keep, taken):
    _, groups, tok, head_size = keep.shape
    whole = pl.BlockSpec(keep.shape, lambda i, *_: (0, 0, 0, 0))
    shape = (tok, 2 * groups * head_size)
    return pl.pallas_call(
        place_kernel,
        grid_spec=pltpu.PrefetchScalarGridSpec(
            num_scalar_prefetch=3,
            grid=(1,),
            in_specs=[whole, whole],
            out_specs=[pl.BlockSpec(shape, lambda i, *_: (0, 0))] * 3,
        ),
        out_shape=[jax.ShapeDtypeStruct(shape, jnp.bfloat16)] * 3,
        compiler_params=pltpu.CompilerParams(vmem_limit_bytes=VMEM_LIMIT),
        cost_estimate=CHEAP,
        name="place_sums",
    )(where, knocked, patch_start, keep, taken)


def place_terms_kernel(size, at_ref, *refs):
    out_ref = refs[-1]
    cols = out_ref.shape[1] // size
    each = (len(refs) - 1) // size
    for n in range(size):
        group = refs[n * each : (n + 1) * each]
        for j in range(size):

            @pl.when(at_ref[n] == j)
            def _():
                total = group[0][...]
                for got in group[1:]:
                    total = total + got[...].astype(jnp.float32)
                out_ref[:, j * cols : (j + 1) * cols] = total


def place_terms(at, groups):
    flat = [x for group in groups for x in group]
    share, cols = flat[0].shape
    shape = (share, len(groups) * cols)
    return pl.pallas_call(
        functools.partial(place_terms_kernel, len(groups)),
        grid_spec=pltpu.PrefetchScalarGridSpec(
            num_scalar_prefetch=1,
            grid=(1,),
            in_specs=[pl.BlockSpec(x.shape, lambda i, c: (0, 0)) for x in flat],
            out_specs=pl.BlockSpec(shape, lambda i, c: (0, 0)),
        ),
        out_shape=jax.ShapeDtypeStruct(shape, jnp.float32),
        compiler_params=pltpu.CompilerParams(vmem_limit_bytes=VMEM_LIMIT),
        cost_estimate=CHEAP,
        name="place_terms",
    )(at, *flat)


def shift(shard, by):
    size = lax.axis_size("ctx")
    return lax.ppermute(shard, "ctx", [(i, i + by) for i in range(size) if 0 <= i + by < size])


def swap_cores(shard, only=None):
    size = lax.axis_size("ctx")
    return lax.ppermute(shard, "ctx", [(i, i ^ 1) for i in range(size) if only is None or i % 2 == only])


def turn(shard, by):
    size = lax.axis_size("head")
    return lax.ppermute(shard, "head", [(i, (i + by) % size) for i in range(size)])


def move(shard, pairs):
    size, n_ctx = lax.axis_size("head"), lax.axis_size("ctx")
    places = [((c + a) * size + i, (c + b) * size + j) for c in range(0, n_ctx, 2) for (a, i), (b, j) in pairs]
    return lax.ppermute(shard, ("ctx", "head"), places)


def after(values, *others):
    return lax.optimization_barrier((values, *others))[0]


def body(queries, cached_keys, values, patch_keys, out_grad, out_weight, knocked, patch_start):
    tok = queries.shape[0]
    kv_local = knocked.shape[0]
    head_size = cached_keys.shape[1] // kv_local
    cols = out_grad.shape[1]
    out_grad = out_grad.T
    n_head, n_ctx = lax.axis_size("head"), lax.axis_size("ctx")
    chips = n_ctx // 2
    place, z = lax.axis_index("ctx"), lax.axis_index("head")
    core, chip = place % 2, place // 2
    low = core == 0
    half_q, half_kv = queries.shape[1] // 2, cached_keys.shape[1] // 2
    dyn = lax.dynamic_slice_in_dim

    partner = swap_cores(out_grad)
    own_block = jnp.stack([jnp.where(low, out_grad, partner), jnp.where(low, partner, out_grad)])
    if n_head == 4:
        up, down = [((0, i), (0, (i + 1) % 4)) for i in range(4)], [((1, i), (1, (i - 1) % 4)) for i in range(4)]
        direct = (move(own_block, up + down),)
        distances, last = [jnp.where(low, 3, 1), jnp.where(low, 1, 3)], 2
    else:
        direct = tuple(turn(own_block, s) for s in range(1, n_head - 1))
        distances, last = [n_head - s for s in range(1, n_head - 1)], 1

    positions = place * tok + jnp.arange(tok, dtype=jnp.int32)
    chosen = (jnp.repeat(knocked, head_size)[None, :] == 1) & (
        positions[:, None] >= jnp.repeat(patch_start, head_size)[None, :]
    )
    patched = jnp.where(chosen, patch_keys, cached_keys)

    def packet_of(which):
        return jnp.concatenate(
            [
                dyn(queries, which * half_q, half_q, 1),
                dyn(patched, which * half_kv, half_kv, 1),
                dyn(values, which * half_kv, half_kv, 1),
            ],
            axis=1,
        )

    mine, other = packet_of(core), swap_cores(packet_of(1 - core))
    packet = jnp.concatenate([jnp.where(low, mine, other), jnp.where(low, other, mine)], axis=0)
    before = shift(packet[:, half_q:], 2)

    order = [0, *distances, last]
    weight_half = dyn(out_weight, core * half_q, half_q, 0)
    weights = [dyn(weight_half, ((z + d) % n_head) * cols, cols, 1) for d in order]
    core_id = core[None].astype(jnp.int32)
    grads = add_grads([own_block], weights[:1], None, jnp.float32)
    before = after(before, grads, weights)

    attention, attended = forward(chip[None].astype(jnp.int32), packet, before, head_size)
    share = out_weight.shape[0] // n_ctx
    parity = attended.reshape(chips // 2, 2, share, 2 * tok)
    kept, given = dyn(parity, core, 1, 1)[:, 0], dyn(parity, 1 - core, 1, 1)[:, 0]
    taken = swap_cores(given)
    by_chip = jnp.concatenate([jnp.where(low, kept, taken), jnp.where(low, taken, kept)], axis=0)
    by_distance = jnp.concatenate([dyn(by_chip, chip ^ s, 1, 0) for s in range(chips)], axis=0)
    by_distance = by_distance.reshape(chips * share, 2 * tok)

    def send_terms(block):
        kept_term, *sent = make_terms(by_distance, block, chips)
        got = [lax.ppermute(x, "ctx", [(i, i ^ (2 * s + 2)) for i in range(n_ctx)]) for s, x in enumerate(sent)]
        return [kept_term, *got], sent

    terms = []

    def wait(value, *others, on=(), since=slice(None)):
        value, _, got = lax.optimization_barrier((value, others, [terms[n][since] for n in on]))
        for n, g in zip(on, got):
            terms[n][since] = g
        return value

    term, sent = send_terms(own_block)
    terms.append(term)
    direct = wait(direct, sent, on=[0], since=slice(1, 3))
    if n_head == 4:
        hops = [((i % 2, i), (i % 2, j)) for i, j in [(0, 1), (1, 0), (2, 3), (3, 2)]]
        final = move(direct[0], hops)
        blocks = [direct[0], swap_cores(direct[0])]
    else:
        final = turn(own_block, -1)
        blocks = list(direct)
    for n, block in enumerate(blocks):
        block = after(block, sent)
        term, sent = send_terms(block)
        terms.append(term)
    grads = add_grads(blocks, weights[1:-1], grads, jnp.float32)

    final = wait(final, grads, sent, on=[0, 1], since=slice(1, None))
    final = wait(final, on=[2], since=slice(1, 3))
    if n_head == 4:
        final = jnp.where(core == 1 - z % 2, final, swap_cores(final))
    term, sent = send_terms(final)
    terms.append(term)
    final = wait(final, sent, on=[2], since=slice(3, None))
    grads = add_grads([final], weights[-1:], grads, jnp.bfloat16)
    grads = wait(grads, on=[3], since=slice(1, None))
    all_groups = (0, packet.shape[1] // (4 * head_size))
    query_low, prev_low, carry = backward(0, all_groups, packet, before, attention, grads, None, head_size)
    from_low = shift(prev_low, -2)
    parts = []
    for g in range(all_groups[1]):
        if g > 0 and g == all_groups[1] - 1:
            grads, from_low = lax.optimization_barrier((grads, from_low))
        parts.append(backward(1, (g, 1), packet, before, attention, grads, carry, head_size))
    query_high = jnp.concatenate([part[0] for part in parts], axis=1)

    weight_grad = place_terms(jnp.stack([(z + d) % n_head for d in order]).astype(jnp.int32), terms)

    query_kept = jnp.where(low, query_low, query_high)
    query_taken = swap_cores(jnp.where(low, query_high, query_low))
    query_grad = jnp.concatenate(
        [jnp.where(low, query_kept, query_taken), jnp.where(low, query_taken, query_kept)], axis=1
    )
    keep, send = close_sums(core_id, from_low, [part[2] for part in parts], [shift(part[1], -2) for part in parts])
    where = jnp.stack([core, place * tok]).astype(jnp.int32)
    key_grad, value_grad, patch_grad = place_sums(where, knocked, patch_start, keep, swap_cores(send))
    return (query_grad, key_grad, value_grad, patch_grad, weight_grad)


def solution(mesh):
    split = P("ctx", "head")
    return jax.shard_map(
        body,
        mesh=mesh,
        in_specs=(split, split, split, split, split, P("head", None), P("head"), P("head")),
        out_specs=(split, split, split, split, P(("head", "ctx"), None)),
        check_vma=False,
    )
```

```python
import functools

import jax
import jax.numpy as jnp
from jax import lax
from jax.experimental import pallas as pl
from jax.experimental.pallas import tpu as pltpu
from jax.sharding import PartitionSpec as P

LOGIT_SCALE = 168.0 ** (-0.5)
EXP2_SCALE = LOGIT_SCALE * 1.4426950408889634
TILE = 256
VMEM_LIMIT = 24 * 1024 * 1024
ATTENTION_VMEM_LIMIT = 48 * 1024 * 1024
CHEAP = pl.CostEstimate(flops=1, bytes_accessed=1, transcendentals=0)

NT = (((1,), (1,)), ((), ()))
NN = (((1,), (0,)), ((), ()))


def dot(a, b, dims=NN):
    return lax.dot_general(a, b, dims, preferred_element_type=jnp.float32)


def stack_heads(pair, head_size):
    return jnp.concatenate([pair[:, :head_size], pair[:, head_size:]], axis=0)


def forward_kernel(chip_ref, q_ref, k_ref, v_ref, pk_ref, pv_ref, p_ref, at_ref, keys, values_t):
    tile = pl.program_id(1)
    rows, head_size = k_ref.shape
    blocks = rows // TILE

    @pl.when(tile == 0)
    def _():
        keys[:rows] = pk_ref[...]
        keys[rows:] = k_ref[...]
        values_t[:, :rows] = pv_ref[...].T
        values_t[:, rows:] = v_ref[...].T

    q = stack_heads(q_ref[...], head_size)
    key_id = lax.broadcasted_iota(jnp.int32, (TILE, 2 * TILE), 0)
    query_id = lax.broadcasted_iota(jnp.int32, (TILE, 2 * TILE), 1) & (TILE - 1)
    first = chip_ref[0] == 0
    top = None
    for b in range(blocks + 1):
        start = pl.multiple_of((tile + b) * TILE, TILE)
        s = dot(keys[pl.ds(start, TILE), :], q, NT)
        if b == 0:
            s = jnp.where(key_id > query_id, s, -jnp.inf)
        if b == blocks:
            s = jnp.where(key_id <= query_id, s, -jnp.inf)
        else:
            s = s + jnp.where(jnp.logical_and(first, tile + b < blocks), -jnp.inf, 0.0)
        p_ref[0, 0, b * TILE : (b + 1) * TILE, :] = s
        here = jnp.max(s, axis=0, keepdims=True)
        top = here if top is None else jnp.maximum(top, here)
    total = None
    for b in range(blocks + 1):
        part = pl.ds(b * TILE, TILE)
        e = jnp.exp2((p_ref[0, 0, part, :] - top) * EXP2_SCALE)
        p_ref[0, 0, part, :] = e
        here = jnp.sum(e, axis=0, keepdims=True)
        total = here if total is None else total + here
    inverse = 1.0 / total
    out = None
    for b in range(blocks + 1):
        part = pl.ds(b * TILE, TILE)
        start = pl.multiple_of((tile + b) * TILE, TILE)
        p = p_ref[0, 0, part, :] * inverse
        p_ref[0, 0, part, :] = p
        term = dot(values_t[:, pl.ds(start, TILE)], p.astype(jnp.bfloat16))
        out = term if out is None else out + term
    at_ref[:head_size] = out[:, :TILE].astype(jnp.bfloat16)
    at_ref[head_size:] = out[:, TILE:].astype(jnp.bfloat16)


def forward(chip, packet, before, head_size):
    rows = packet.shape[0]
    groups = packet.shape[1] // (4 * head_size)
    tiles = rows // TILE
    span = rows + TILE
    grid_spec = pltpu.PrefetchScalarGridSpec(
        num_scalar_prefetch=1,
        grid=(groups, tiles),
        in_specs=[
            pl.BlockSpec((TILE, 2 * head_size), lambda g, i, c: (i, g)),
            pl.BlockSpec((rows, head_size), lambda g, i, c: (0, 2 * groups + g)),
            pl.BlockSpec((rows, head_size), lambda g, i, c: (0, 3 * groups + g)),
            pl.BlockSpec((rows, head_size), lambda g, i, c: (0, g)),
            pl.BlockSpec((rows, head_size), lambda g, i, c: (0, groups + g)),
        ],
        out_specs=[
            pl.BlockSpec((1, 1, span, 2 * TILE), lambda g, i, c: (g, i, 0, 0)),
            pl.BlockSpec((2 * head_size, TILE), lambda g, i, c: (g, i)),
        ],
        scratch_shapes=[
            pltpu.VMEM((2 * rows, head_size), jnp.bfloat16),
            pltpu.VMEM((head_size, 2 * rows), jnp.bfloat16),
        ],
    )
    return pl.pallas_call(
        forward_kernel,
        grid_spec=grid_spec,
        out_shape=[
            jax.ShapeDtypeStruct((groups, tiles, span, 2 * TILE), jnp.float32),
            jax.ShapeDtypeStruct((groups * 2 * head_size, rows), jnp.bfloat16),
        ],
        compiler_params=pltpu.CompilerParams(vmem_limit_bytes=ATTENTION_VMEM_LIMIT),
        cost_estimate=CHEAP,
        name="attention_forward",
    )(chip, packet, packet, packet, before, before)


def backward_kernel(
    phase, q_ref, k_ref, v_ref, pk_ref, pv_ref, p_ref, do_ref, carry_ref, dq_ref, dprev_ref, keep_ref, keys_t, values, dk, dv, dp
):
    tile = pl.program_id(1)
    rows, head_size = k_ref.shape
    blocks = rows // TILE
    half = rows // 2
    old = rows - phase * half

    @pl.when(tile == 0)
    def _():
        keys_t[:, :old] = pk_ref[rows - old :, :].T
        keys_t[:, old:] = k_ref[: half + rows - old, :].T
        values[:old] = pv_ref[rows - old :, :]
        values[old:] = v_ref[: half + rows - old, :]
        if phase == 0:
            dk[...] = jnp.zeros_like(dk)
            dv[...] = jnp.zeros_like(dv)
        else:
            dk[:rows] = carry_ref[0, 0]
            dv[:rows] = carry_ref[1, 0]
            dk[rows:] = jnp.zeros((half, head_size), jnp.float32)
            dv[rows:] = jnp.zeros((half, head_size), jnp.float32)

    q = stack_heads(q_ref[...], head_size)
    do = jnp.concatenate([do_ref[:head_size], do_ref[head_size:]], axis=1)
    centre = None
    for b in range(blocks + 1):
        start = pl.multiple_of((tile + b) * TILE, TILE)
        part = pl.ds(b * TILE, TILE)
        p = p_ref[0, 0, part, :]
        grad = dot(values[pl.ds(start, TILE), :], do)
        dp[part, :] = grad
        here = jnp.sum(p * grad, axis=0, keepdims=True)
        centre = here if centre is None else centre + here
        dv[pl.ds(start, TILE), :] += dot(p.astype(jnp.bfloat16), do, NT)
    out = None
    for b in range(blocks + 1):
        start = pl.multiple_of((tile + b) * TILE, TILE)
        part = pl.ds(b * TILE, TILE)
        ds = (p_ref[0, 0, part, :] * (dp[part, :] - centre)).astype(jnp.bfloat16)
        dk[pl.ds(start, TILE), :] += dot(ds, q)
        term = dot(keys_t[:, pl.ds(start, TILE)], ds)
        out = term if out is None else out + term
    out = out * LOGIT_SCALE
    dq_ref[:, :head_size] = out[:, :TILE].T.astype(jnp.bfloat16)
    dq_ref[:, head_size:] = out[:, TILE:].T.astype(jnp.bfloat16)

    @pl.when(tile == pl.num_programs(1) - 1)
    def _():
        dprev_ref[0, 0] = (dk[:half] * LOGIT_SCALE).astype(jnp.bfloat16)
        dprev_ref[1, 0] = dv[:half].astype(jnp.bfloat16)
        keep_ref[0, 0] = dk[half:]
        keep_ref[1, 0] = dv[half:]


def backward(phase, members, packet, before, attention, out_grads, carry, head_size):
    rows = packet.shape[0]
    groups = packet.shape[1] // (4 * head_size)
    g0, count = members
    tiles = rows // TILE // 2
    half = rows // 2
    span = rows + TILE
    first = phase * tiles
    if carry is None:
        carry = jnp.zeros((2, 1, 8, head_size), jnp.float32)
        carry_spec = pl.BlockSpec((2, 1, 8, head_size), lambda g, i: (0, 0, 0, 0))
    else:
        carry_spec = pl.BlockSpec((2, 1, rows, head_size), lambda g, i: (0, g0 + g, 0, 0))
    return pl.pallas_call(
        functools.partial(backward_kernel, phase),
        grid=(count, tiles),
        in_specs=[
            pl.BlockSpec((TILE, 2 * head_size), lambda g, i: (first + i, g0 + g)),
            pl.BlockSpec((rows, head_size), lambda g, i: (0, 2 * groups + g0 + g)),
            pl.BlockSpec((rows, head_size), lambda g, i: (0, 3 * groups + g0 + g)),
            pl.BlockSpec((rows, head_size), lambda g, i: (0, g0 + g)),
            pl.BlockSpec((rows, head_size), lambda g, i: (0, groups + g0 + g)),
            pl.BlockSpec((1, 1, span, 2 * TILE), lambda g, i: (g0 + g, first + i, 0, 0)),
            pl.BlockSpec((2 * head_size, TILE), lambda g, i: (g0 + g, first + i)),
            carry_spec,
        ],
        out_specs=[
            pl.BlockSpec((TILE, 2 * head_size), lambda g, i: (i, g)),
            pl.BlockSpec((2, 1, half, head_size), lambda g, i: (0, g, 0, 0)),
            pl.BlockSpec((2, 1, rows, head_size), lambda g, i: (0, g, 0, 0)),
        ],
        out_shape=[
            jax.ShapeDtypeStruct((half, count * 2 * head_size), jnp.bfloat16),
            jax.ShapeDtypeStruct((2, count, half, head_size), jnp.bfloat16),
            jax.ShapeDtypeStruct((2, count, rows, head_size), jnp.float32),
        ],
        scratch_shapes=[
            pltpu.VMEM((head_size, rows + half), jnp.bfloat16),
            pltpu.VMEM((rows + half, head_size), jnp.bfloat16),
            pltpu.VMEM((rows + half, head_size), jnp.float32),
            pltpu.VMEM((rows + half, head_size), jnp.float32),
            pltpu.VMEM((span, 2 * TILE), jnp.float32),
        ],
        compiler_params=pltpu.CompilerParams(vmem_limit_bytes=ATTENTION_VMEM_LIMIT),
        cost_estimate=CHEAP,
        name="attention_backward",
    )(packet, packet, packet, before, before, attention, out_grads, carry)


def grads_kernel(number, *refs):
    blocks, weights = refs[:number], refs[number : 2 * number]
    total = None
    for block, weight in zip(blocks, weights):
        term = dot(weight[...], block[0])
        total = term if total is None else total + term
    for old in refs[2 * number : -1]:
        total = total + old[...]
    refs[-1][...] = total.astype(refs[-1].dtype)


def add_grads(blocks, weights, total, dtype):
    _, cols, tok = blocks[0].shape
    width = weights[0].shape[0]
    tiles = tok // TILE
    tile_spec = pl.BlockSpec((width, TILE), lambda i: (0, i))
    number = len(blocks)
    return pl.pallas_call(
        functools.partial(grads_kernel, number),
        grid=(2 * tiles,),
        in_specs=[pl.BlockSpec((1, cols, TILE), lambda i: (i // tiles, 0, i % tiles))] * number
        + [pl.BlockSpec((width, cols), lambda i: (0, 0))] * number
        + ([] if total is None else [tile_spec]),
        out_specs=tile_spec,
        out_shape=jax.ShapeDtypeStruct((width, 2 * tok), dtype),
        compiler_params=pltpu.CompilerParams(vmem_limit_bytes=VMEM_LIMIT),
        cost_estimate=CHEAP,
        name="out_grads",
    )(*blocks, *weights, *([] if total is None else [total]))


def terms_kernel(orders, count, rows_ref, *refs):
    number = len(orders)
    blocks, waiting = refs[:number], refs[number : number + 3 * count]
    outs, passed = refs[number + 3 * count : number + 3 * count + 3 * number], refs[number + 3 * count + 3 * number :]
    for n in range(count):
        keep, near, got = waiting[3 * n : 3 * n + 3]
        cols = keep.shape[1]
        passed[2 * n][...] = keep[...] + got[:, :cols].astype(jnp.float32)
        passed[2 * n + 1][...] = (near[...] + got[:, cols:].astype(jnp.float32)).astype(jnp.bfloat16)
    for n, (block, first) in enumerate(zip(blocks, orders)):
        _, cols, tok = block.shape
        share = rows_ref.shape[0] // 4
        keep, near, send = outs[3 * n : 3 * n + 3]
        for at in range(0, cols, TILE):
            end = min(at + TILE, cols)
            term = dot(rows_ref[:, :tok], block[0, at:end, :], NT) + dot(rows_ref[:, tok:], block[1, at:end, :], NT)
            parts = [term[s * share : (s + 1) * share] for s in range(4)]
            keep[:, at:end] = parts[0]
            near[:, at:end] = parts[3 - first]
            send[:, at:end] = parts[first].astype(jnp.bfloat16)
            send[:, cols + at : cols + end] = parts[3].astype(jnp.bfloat16)


def make_terms(rows, blocks, orders, waiting):
    share = rows.shape[0] // 4
    flat = [x for group in waiting for x in group]
    whole = lambda x: pl.BlockSpec(x.shape, lambda i: (0,) * len(x.shape))
    shapes = []
    for block in blocks:
        cols = block.shape[1]
        shapes += [jax.ShapeDtypeStruct((share, cols), jnp.float32)] * 2
        shapes.append(jax.ShapeDtypeStruct((share, 2 * cols), jnp.bfloat16))
    for keep, _, _ in waiting:
        shapes += [jax.ShapeDtypeStruct(keep.shape, jnp.float32), jax.ShapeDtypeStruct(keep.shape, jnp.bfloat16)]
    out = pl.pallas_call(
        functools.partial(terms_kernel, orders, len(waiting)),
        grid=(1,),
        in_specs=[whole(x) for x in (rows, *blocks, *flat)],
        out_specs=[whole(x) for x in shapes],
        out_shape=shapes,
        compiler_params=pltpu.CompilerParams(vmem_limit_bytes=VMEM_LIMIT),
        cost_estimate=CHEAP,
        name="weight_terms",
    )(rows, *blocks, *flat)
    cut = 3 * len(blocks)
    return [list(out[n : n + 3]) for n in range(0, cut, 3)], [list(out[n : n + 2]) for n in range(cut, len(out), 2)]


def close_kernel(groups, core_ref, from_low_ref, *refs):
    owns, highs, (keep_ref, send_ref) = refs[:groups], refs[groups : 2 * groups], refs[2 * groups :]
    half = from_low_ref.shape[2]

    def write(low_ref, high_ref):
        for part in range(2):
            scale = LOGIT_SCALE if part == 0 else 1.0
            for g in range(groups):
                low = owns[g][part, 0, :half] * scale + from_low_ref[part, g].astype(jnp.float32)
                high = owns[g][part, 0, half:] * scale + highs[g][part, 0].astype(jnp.float32)
                low_ref[part, g] = low.astype(jnp.bfloat16)
                high_ref[part, g] = high.astype(jnp.bfloat16)

    @pl.when(core_ref[0] == 0)
    def _():
        write(keep_ref, send_ref)

    @pl.when(core_ref[0] == 1)
    def _():
        write(send_ref, keep_ref)


def close_sums(core, from_low, owns, highs):
    whole = lambda x: pl.BlockSpec(x.shape, lambda i, c: (0,) * x.ndim)
    out = jax.ShapeDtypeStruct(from_low.shape, jnp.bfloat16)
    return pl.pallas_call(
        functools.partial(close_kernel, len(owns)),
        grid_spec=pltpu.PrefetchScalarGridSpec(
            num_scalar_prefetch=1,
            grid=(1,),
            in_specs=[whole(x) for x in (from_low, *owns, *highs)],
            out_specs=[whole(out), whole(out)],
        ),
        out_shape=[out, out],
        compiler_params=pltpu.CompilerParams(vmem_limit_bytes=VMEM_LIMIT),
        cost_estimate=CHEAP,
        name="close_sums",
    )(core, from_low, *owns, *highs)


def place_kernel(where_ref, knocked_ref, start_ref, keep_ref, taken_ref, key_ref, value_ref, patch_ref):
    groups, tok, head_size = keep_ref.shape[1:]
    core, row_start = where_ref[0], where_ref[1]
    positions = row_start + lax.broadcasted_iota(jnp.int32, (tok, head_size), 0)
    for head in range(2 * groups):
        own = core == head // groups
        at = slice(head * head_size, (head + 1) * head_size)
        both = [
            jnp.where(own, keep_ref[part, head % groups].astype(jnp.float32), taken_ref[part, head % groups].astype(jnp.float32))
            for part in range(2)
        ]
        chosen = jnp.logical_and(knocked_ref[head] == 1, positions >= start_ref[head])
        key_ref[:, at] = jnp.where(chosen, 0.0, both[0]).astype(jnp.bfloat16)
        patch_ref[:, at] = jnp.where(chosen, both[0], 0.0).astype(jnp.bfloat16)
        value_ref[:, at] = both[1].astype(jnp.bfloat16)


def place_sums(where, knocked, patch_start, keep, taken):
    _, groups, tok, head_size = keep.shape
    whole = pl.BlockSpec(keep.shape, lambda i, *_: (0, 0, 0, 0))
    shape = (tok, 2 * groups * head_size)
    return pl.pallas_call(
        place_kernel,
        grid_spec=pltpu.PrefetchScalarGridSpec(
            num_scalar_prefetch=3,
            grid=(1,),
            in_specs=[whole, whole],
            out_specs=[pl.BlockSpec(shape, lambda i, *_: (0, 0))] * 3,
        ),
        out_shape=[jax.ShapeDtypeStruct(shape, jnp.bfloat16)] * 3,
        compiler_params=pltpu.CompilerParams(vmem_limit_bytes=VMEM_LIMIT),
        cost_estimate=CHEAP,
        name="place_sums",
    )(where, knocked, patch_start, keep, taken)


def place_terms_kernel(at_ref, *refs):
    out_ref = refs[-1]
    size = (len(refs) - 1) // 2
    cols = refs[0].shape[1]
    for n in range(size):
        for j in range(size):

            @pl.when(at_ref[n] == j)
            def _():
                out_ref[:, j * cols : (j + 1) * cols] = refs[2 * n][...] + refs[2 * n + 1][...].astype(jnp.float32)


def place_terms(at, terms):
    flat = [x for term in terms for x in term]
    share, cols = flat[0].shape
    return pl.pallas_call(
        place_terms_kernel,
        grid_spec=pltpu.PrefetchScalarGridSpec(
            num_scalar_prefetch=1,
            grid=(1,),
            in_specs=[pl.BlockSpec(x.shape, lambda i, c: (0, 0)) for x in flat],
            out_specs=pl.BlockSpec((share, cols * len(terms)), lambda i, c: (0, 0)),
        ),
        out_shape=jax.ShapeDtypeStruct((share, cols * len(terms)), jnp.float32),
        compiler_params=pltpu.CompilerParams(vmem_limit_bytes=VMEM_LIMIT),
        cost_estimate=CHEAP,
        name="place_terms",
    )(at, *flat)


def shift(shard, by):
    size = lax.axis_size("ctx")
    return lax.ppermute(shard, "ctx", [(i, i + by) for i in range(size) if 0 <= i + by < size])


def swap_cores(shard, only=None):
    size = lax.axis_size("ctx")
    return lax.ppermute(shard, "ctx", [(i, i ^ 1) for i in range(size) if only is None or i % 2 == only])


def turn(shard, by):
    size = lax.axis_size("head")
    return lax.ppermute(shard, "head", [(i, (i + by) % size) for i in range(size)])


def move(shard, pairs):
    size, n_ctx = lax.axis_size("head"), lax.axis_size("ctx")
    places = [((c + a) * size + i, (c + b) * size + j) for c in range(0, n_ctx, 2) for (a, i), (b, j) in pairs]
    return lax.ppermute(shard, ("ctx", "head"), places)


def after(values, *others):
    return lax.optimization_barrier((values, *others))[0]


def body(queries, cached_keys, values, patch_keys, out_grad, out_weight, knocked, patch_start):
    tok = queries.shape[0]
    kv_local = knocked.shape[0]
    head_size = cached_keys.shape[1] // kv_local
    cols = out_grad.shape[1]
    out_grad = out_grad.T
    n_head, n_ctx = lax.axis_size("head"), lax.axis_size("ctx")
    chips = n_ctx // 2
    place, z = lax.axis_index("ctx"), lax.axis_index("head")
    core, chip = place % 2, place // 2
    low = core == 0
    half_q, half_kv = queries.shape[1] // 2, cached_keys.shape[1] // 2
    dyn = lax.dynamic_slice_in_dim

    fast = n_head == 4 and chips == 4
    partner = swap_cores(out_grad)
    own_block = jnp.stack([jnp.where(low, out_grad, partner), jnp.where(low, partner, out_grad)])
    if fast:
        up, down = [((0, i), (0, (i + 1) % 4)) for i in range(4)], [((1, i), (1, (i - 1) % 4)) for i in range(4)]
        direct = move(own_block, up + down)
        order = [0, jnp.where(low, 3, 1), jnp.where(low, 1, 3), 2]
    else:
        direct = [turn(own_block, s) for s in range(1, n_head)]
        order = [(n_head - s) % n_head for s in range(n_head)]

    positions = place * tok + jnp.arange(tok, dtype=jnp.int32)
    chosen = (jnp.repeat(knocked, head_size)[None, :] == 1) & (
        positions[:, None] >= jnp.repeat(patch_start, head_size)[None, :]
    )
    patched = jnp.where(chosen, patch_keys, cached_keys)

    def packet_of(which):
        return jnp.concatenate(
            [
                dyn(queries, which * half_q, half_q, 1),
                dyn(patched, which * half_kv, half_kv, 1),
                dyn(values, which * half_kv, half_kv, 1),
            ],
            axis=1,
        )

    mine, other = packet_of(core), swap_cores(packet_of(1 - core))
    packet = jnp.concatenate([jnp.where(low, mine, other), jnp.where(low, other, mine)], axis=0)
    before = shift(packet[:, half_q:], 2)

    weight_half = dyn(out_weight, core * half_q, half_q, 0)
    weights = [dyn(weight_half, ((z + d) % n_head) * cols, cols, 1) for d in order]
    core_id = core[None].astype(jnp.int32)
    grads = add_grads([own_block], weights[:1], None, jnp.float32)
    before = after(before, grads, weights)

    attention, attended = forward(chip[None].astype(jnp.int32), packet, before, head_size)
    if fast:
        share = out_weight.shape[0] // n_ctx
        parity = attended.reshape(chips // 2, 2, share, 2 * tok)
        kept, given = dyn(parity, core, 1, 1)[:, 0], dyn(parity, 1 - core, 1, 1)[:, 0]
        taken = swap_cores(given)
        by_chip = jnp.concatenate([jnp.where(low, kept, taken), jnp.where(low, taken, kept)], axis=0)
        by_distance = jnp.concatenate([dyn(by_chip, chip ^ s, 1, 0) for s in range(chips)], axis=0)
        by_distance = by_distance.reshape(chips * share, 2 * tok)

        def exchange(shard, distance):
            return lax.ppermute(shard, "ctx", [(i, i ^ (2 * distance)) for i in range(n_ctx)])

        direct = after(direct, by_distance)
        final = move(direct, [((i % 2, i), (i % 2, j)) for i, j in [(0, 1), (1, 0), (2, 3), (3, 2)]])
        blocks = [direct, swap_cores(direct)]
        (own_terms, up_terms, down_terms), _ = make_terms(by_distance, [own_block, *blocks], (1, 1, 2), [])
        own_got, up_got, down_got = exchange(own_terms[2], 1), exchange(up_terms[2], 1), exchange(down_terms[2], 2)
        grads = add_grads(blocks, weights[1:3], grads, jnp.float32)

        final, own_got, down_got, grads = lax.optimization_barrier((final, own_got, down_got, grads))
        final = jnp.where(core == 1 - z % 2, final, swap_cores(final))
        (last_terms,), (own_sum, down_sum) = make_terms(
            by_distance, [final], (2,), [(*own_terms[:2], own_got), (*down_terms[:2], down_got)]
        )
        last_got = exchange(last_terms[2], 2)
        own_sum[1], down_sum[1] = exchange(own_sum[1], 2), exchange(down_sum[1], 1)
        final, _, up_got = lax.optimization_barrier((final, last_terms[2], up_got))
        grads = add_grads([final], weights[3:], grads, jnp.bfloat16)
    else:
        blocks = [own_block, *direct]
        grads = add_grads(blocks[1:], weights[1:], grads, jnp.float32).astype(jnp.bfloat16)
        term = jnp.stack([sum(dot(attended[:, i * tok : (i + 1) * tok], x[i], NT) for i in (0, 1)) for x in blocks])
        term = jnp.concatenate([dyn(term, (z - j) % n_head, 1, 0)[0] for j in range(n_head)], axis=1)
        term = jnp.concatenate([jnp.where(low, term, 0.0), jnp.where(low, 0.0, term)], axis=0)
        weight_grad = lax.psum_scatter(term, "ctx", scatter_dimension=0, tiled=True)
    all_groups = (0, packet.shape[1] // (4 * head_size))
    query_low, prev_low, carry = backward(0, all_groups, packet, before, attention, grads, None, head_size)
    if fast:
        sent = (own_sum[1], down_sum[1])
        query_low, prev_low, carry, last_got, sent = lax.optimization_barrier(
            (query_low, prev_low, carry, last_got, sent)
        )
        own_sum[1], down_sum[1] = sent
        waiting = [(*up_terms[:2], up_got), (*last_terms[:2], last_got)]
        _, (up_sum, last_sum) = make_terms(by_distance, [], (), waiting)
        prev_low = after(prev_low, last_sum[1])
        up_sum[1], last_sum[1] = exchange(up_sum[1], 2), exchange(last_sum[1], 1)
    from_low = shift(prev_low, -2)
    parts, from_high = [], []
    for g in range(all_groups[1]):
        part = backward(1, (g, 1), packet, before, attention, grads, carry, head_size)
        if g > 0:
            part, from_low, from_high = lax.optimization_barrier((part, from_low, from_high))
        parts.append(part)
        from_high.append(shift(part[1], -2))
    query_high = jnp.concatenate([part[0] for part in parts], axis=1)

    if fast:
        at = jnp.stack([(z + d) % n_head for d in order]).astype(jnp.int32)
        weight_grad = place_terms(at, [own_sum, up_sum, down_sum, last_sum])

    query_kept = jnp.where(low, query_low, query_high)
    query_taken = swap_cores(jnp.where(low, query_high, query_low))
    query_grad = jnp.concatenate(
        [jnp.where(low, query_kept, query_taken), jnp.where(low, query_taken, query_kept)], axis=1
    )
    from_high = after(from_high, weight_grad)
    keep, send = close_sums(core_id, from_low, [part[2] for part in parts], from_high)
    rows_at = jnp.stack([core, place * tok]).astype(jnp.int32)
    taken = after(swap_cores(send), query_grad)
    key_grad, value_grad, patch_grad = place_sums(rows_at, knocked, patch_start, keep, taken)
    return (query_grad, key_grad, value_grad, patch_grad, weight_grad)


def solution(mesh):
    split = P("ctx", "head")
    return jax.shard_map(
        body,
        mesh=mesh,
        in_specs=(split, split, split, split, split, P("head", None), P("head"), P("head")),
        out_specs=(split, split, split, split, P(("head", "ctx"), None)),
        check_vma=False,
    )
```

```python
import functools

import jax
import jax.numpy as jnp
from jax import lax
from jax.experimental import pallas as pl
from jax.experimental.pallas import tpu as pltpu
from jax.sharding import PartitionSpec as P

LOGIT_SCALE = 168.0 ** (-0.5)
EXP2_SCALE = LOGIT_SCALE * 1.4426950408889634
TILE = 256
VMEM_LIMIT = 24 * 1024 * 1024
ATTENTION_VMEM_LIMIT = 48 * 1024 * 1024
CHEAP = pl.CostEstimate(flops=1, bytes_accessed=1, transcendentals=0)

NT = (((1,), (1,)), ((), ()))
NN = (((1,), (0,)), ((), ()))


def dot(a, b, dims=NN):
    return lax.dot_general(a, b, dims, preferred_element_type=jnp.float32)


def stack_heads(pair, head_size):
    return jnp.concatenate([pair[:, :head_size], pair[:, head_size:]], axis=0)


def forward_kernel(chip_ref, q_ref, k_ref, v_ref, pk_ref, pv_ref, p_ref, at_ref, keys, values_t):
    tile = pl.program_id(1)
    rows, head_size = k_ref.shape
    blocks = rows // TILE

    @pl.when(tile == 0)
    def _():
        keys[:rows] = pk_ref[...]
        keys[rows:] = k_ref[...]
        values_t[:, :rows] = pv_ref[...].T
        values_t[:, rows:] = v_ref[...].T

    q = stack_heads(q_ref[...], head_size)
    key_id = lax.broadcasted_iota(jnp.int32, (TILE, 2 * TILE), 0)
    query_id = lax.broadcasted_iota(jnp.int32, (TILE, 2 * TILE), 1) & (TILE - 1)
    first = chip_ref[0] == 0
    top = None
    for b in range(blocks + 1):
        start = pl.multiple_of((tile + b) * TILE, TILE)
        s = dot(keys[pl.ds(start, TILE), :], q, NT)
        if b == 0:
            s = jnp.where(key_id > query_id, s, -jnp.inf)
        if b == blocks:
            s = jnp.where(key_id <= query_id, s, -jnp.inf)
        else:
            s = s + jnp.where(jnp.logical_and(first, tile + b < blocks), -jnp.inf, 0.0)
        p_ref[0, 0, b * TILE : (b + 1) * TILE, :] = s
        here = jnp.max(s, axis=0, keepdims=True)
        top = here if top is None else jnp.maximum(top, here)
    total = None
    for b in range(blocks + 1):
        part = pl.ds(b * TILE, TILE)
        e = jnp.exp2((p_ref[0, 0, part, :] - top) * EXP2_SCALE)
        p_ref[0, 0, part, :] = e
        here = jnp.sum(e, axis=0, keepdims=True)
        total = here if total is None else total + here
    inverse = 1.0 / total
    out = None
    for b in range(blocks + 1):
        part = pl.ds(b * TILE, TILE)
        start = pl.multiple_of((tile + b) * TILE, TILE)
        p = p_ref[0, 0, part, :] * inverse
        p_ref[0, 0, part, :] = p
        term = dot(values_t[:, pl.ds(start, TILE)], p.astype(jnp.bfloat16))
        out = term if out is None else out + term
    at_ref[:head_size] = out[:, :TILE].astype(jnp.bfloat16)
    at_ref[head_size:] = out[:, TILE:].astype(jnp.bfloat16)


def forward(chip, packet, before, head_size):
    rows = packet.shape[0]
    groups = packet.shape[1] // (4 * head_size)
    tiles = rows // TILE
    span = rows + TILE
    grid_spec = pltpu.PrefetchScalarGridSpec(
        num_scalar_prefetch=1,
        grid=(groups, tiles),
        in_specs=[
            pl.BlockSpec((TILE, 2 * head_size), lambda g, i, c: (i, g)),
            pl.BlockSpec((rows, head_size), lambda g, i, c: (0, 2 * groups + g)),
            pl.BlockSpec((rows, head_size), lambda g, i, c: (0, 3 * groups + g)),
            pl.BlockSpec((rows, head_size), lambda g, i, c: (0, g)),
            pl.BlockSpec((rows, head_size), lambda g, i, c: (0, groups + g)),
        ],
        out_specs=[
            pl.BlockSpec((1, 1, span, 2 * TILE), lambda g, i, c: (g, i, 0, 0)),
            pl.BlockSpec((2 * head_size, TILE), lambda g, i, c: (g, i)),
        ],
        scratch_shapes=[
            pltpu.VMEM((2 * rows, head_size), jnp.bfloat16),
            pltpu.VMEM((head_size, 2 * rows), jnp.bfloat16),
        ],
    )
    return pl.pallas_call(
        forward_kernel,
        grid_spec=grid_spec,
        out_shape=[
            jax.ShapeDtypeStruct((groups, tiles, span, 2 * TILE), jnp.float32),
            jax.ShapeDtypeStruct((groups * 2 * head_size, rows), jnp.bfloat16),
        ],
        compiler_params=pltpu.CompilerParams(vmem_limit_bytes=ATTENTION_VMEM_LIMIT),
        cost_estimate=CHEAP,
        name="attention_forward",
    )(chip, packet, packet, packet, before, before)


def backward_kernel(
    phase, q_ref, k_ref, v_ref, pk_ref, pv_ref, p_ref, do_ref, carry_ref, dq_ref, dprev_ref, keep_ref, keys_t, values, dk, dv, dp
):
    tile = pl.program_id(1)
    rows, head_size = k_ref.shape
    blocks = rows // TILE
    half = rows // 2
    old = rows - phase * half

    @pl.when(tile == 0)
    def _():
        keys_t[:, :old] = pk_ref[rows - old :, :].T
        keys_t[:, old:] = k_ref[: half + rows - old, :].T
        values[:old] = pv_ref[rows - old :, :]
        values[old:] = v_ref[: half + rows - old, :]
        if phase == 0:
            dk[...] = jnp.zeros_like(dk)
            dv[...] = jnp.zeros_like(dv)
        else:
            dk[:rows] = carry_ref[0, 0]
            dv[:rows] = carry_ref[1, 0]
            dk[rows:] = jnp.zeros((half, head_size), jnp.float32)
            dv[rows:] = jnp.zeros((half, head_size), jnp.float32)

    q = stack_heads(q_ref[...], head_size)
    do = jnp.concatenate([do_ref[:head_size], do_ref[head_size:]], axis=1)
    centre = None
    for b in range(blocks + 1):
        start = pl.multiple_of((tile + b) * TILE, TILE)
        part = pl.ds(b * TILE, TILE)
        p = p_ref[0, 0, part, :]
        grad = dot(values[pl.ds(start, TILE), :], do)
        dp[part, :] = grad
        here = jnp.sum(p * grad, axis=0, keepdims=True)
        centre = here if centre is None else centre + here
        dv[pl.ds(start, TILE), :] += dot(p.astype(jnp.bfloat16), do, NT)
    out = None
    for b in range(blocks + 1):
        start = pl.multiple_of((tile + b) * TILE, TILE)
        part = pl.ds(b * TILE, TILE)
        ds = (p_ref[0, 0, part, :] * (dp[part, :] - centre)).astype(jnp.bfloat16)
        dk[pl.ds(start, TILE), :] += dot(ds, q)
        term = dot(keys_t[:, pl.ds(start, TILE)], ds)
        out = term if out is None else out + term
    out = out * LOGIT_SCALE
    dq_ref[:, :head_size] = out[:, :TILE].T.astype(jnp.bfloat16)
    dq_ref[:, head_size:] = out[:, TILE:].T.astype(jnp.bfloat16)

    @pl.when(tile == pl.num_programs(1) - 1)
    def _():
        dprev_ref[0, 0] = (dk[:half] * LOGIT_SCALE).astype(jnp.bfloat16)
        dprev_ref[1, 0] = dv[:half].astype(jnp.bfloat16)
        keep_ref[0, 0] = dk[half:]
        keep_ref[1, 0] = dv[half:]


def backward(phase, members, packet, before, attention, out_grads, carry, head_size):
    rows = packet.shape[0]
    groups = packet.shape[1] // (4 * head_size)
    g0, count = members
    tiles = rows // TILE // 2
    half = rows // 2
    span = rows + TILE
    first = phase * tiles
    if carry is None:
        carry = jnp.zeros((2, 1, 8, head_size), jnp.float32)
        carry_spec = pl.BlockSpec((2, 1, 8, head_size), lambda g, i: (0, 0, 0, 0))
    else:
        carry_spec = pl.BlockSpec((2, 1, rows, head_size), lambda g, i: (0, g0 + g, 0, 0))
    return pl.pallas_call(
        functools.partial(backward_kernel, phase),
        grid=(count, tiles),
        in_specs=[
            pl.BlockSpec((TILE, 2 * head_size), lambda g, i: (first + i, g0 + g)),
            pl.BlockSpec((rows, head_size), lambda g, i: (0, 2 * groups + g0 + g)),
            pl.BlockSpec((rows, head_size), lambda g, i: (0, 3 * groups + g0 + g)),
            pl.BlockSpec((rows, head_size), lambda g, i: (0, g0 + g)),
            pl.BlockSpec((rows, head_size), lambda g, i: (0, groups + g0 + g)),
            pl.BlockSpec((1, 1, span, 2 * TILE), lambda g, i: (g0 + g, first + i, 0, 0)),
            pl.BlockSpec((2 * head_size, TILE), lambda g, i: (g0 + g, first + i)),
            carry_spec,
        ],
        out_specs=[
            pl.BlockSpec((TILE, 2 * head_size), lambda g, i: (i, g)),
            pl.BlockSpec((2, 1, half, head_size), lambda g, i: (0, g, 0, 0)),
            pl.BlockSpec((2, 1, rows, head_size), lambda g, i: (0, g, 0, 0)),
        ],
        out_shape=[
            jax.ShapeDtypeStruct((half, count * 2 * head_size), jnp.bfloat16),
            jax.ShapeDtypeStruct((2, count, half, head_size), jnp.bfloat16),
            jax.ShapeDtypeStruct((2, count, rows, head_size), jnp.float32),
        ],
        scratch_shapes=[
            pltpu.VMEM((head_size, rows + half), jnp.bfloat16),
            pltpu.VMEM((rows + half, head_size), jnp.bfloat16),
            pltpu.VMEM((rows + half, head_size), jnp.float32),
            pltpu.VMEM((rows + half, head_size), jnp.float32),
            pltpu.VMEM((span, 2 * TILE), jnp.float32),
        ],
        compiler_params=pltpu.CompilerParams(vmem_limit_bytes=ATTENTION_VMEM_LIMIT),
        cost_estimate=CHEAP,
        name="attention_backward",
    )(packet, packet, packet, before, before, attention, out_grads, carry)


def grads_kernel(number, halves, *refs):
    blocks, weights = refs[:number], refs[number : 2 * number]
    total = None
    others = refs[2 * number : 3 * number] if halves else [None] * number
    for block, other, weight in zip(blocks, others, weights):
        term = dot(weight[...], block[0] if other is None else block[0] + other[0])
        total = term if total is None else total + term
    for old in refs[(3 if halves else 2) * number : -1]:
        total = total + old[...]
    refs[-1][...] = total.astype(refs[-1].dtype)


def add_grads(blocks, weights, total, dtype, others=()):
    _, cols, tok = blocks[0].shape
    width = weights[0].shape[0]
    tiles = tok // TILE
    tile_spec = pl.BlockSpec((width, TILE), lambda i: (0, i))
    number = len(blocks)
    return pl.pallas_call(
        functools.partial(grads_kernel, number, len(others) > 0),
        grid=(2 * tiles,),
        in_specs=[pl.BlockSpec((1, cols, TILE), lambda i: (i // tiles, 0, i % tiles))] * number
        + [pl.BlockSpec((width, cols), lambda i: (0, 0))] * number
        + [pl.BlockSpec((1, cols, TILE), lambda i: (i // tiles, 0, i % tiles))] * len(others)
        + ([] if total is None else [tile_spec]),
        out_specs=tile_spec,
        out_shape=jax.ShapeDtypeStruct((width, 2 * tok), dtype),
        compiler_params=pltpu.CompilerParams(vmem_limit_bytes=VMEM_LIMIT),
        cost_estimate=CHEAP,
        name="out_grads",
    )(*blocks, *weights, *others, *([] if total is None else [total]))


def terms_kernel(orders, count, halves, rows_ref, *refs):
    number = len(orders)
    others, refs = (refs[:number], refs[number:]) if halves else ([None] * number, refs)
    blocks, waiting = refs[:number], refs[number : number + 3 * count]
    outs, passed = refs[number + 3 * count : number + 3 * count + 3 * number], refs[number + 3 * count + 3 * number :]
    for n in range(count):
        keep, near, got = waiting[3 * n : 3 * n + 3]
        cols = keep.shape[1]
        passed[2 * n][...] = keep[...] + got[:, :cols].astype(jnp.float32)
        passed[2 * n + 1][...] = (near[...] + got[:, cols:].astype(jnp.float32)).astype(jnp.bfloat16)
    for n, (block, other, first) in enumerate(zip(blocks, others, orders)):
        _, cols, tok = block.shape
        share = rows_ref.shape[0] // 4
        keep, near, send = outs[3 * n : 3 * n + 3]
        for at in range(0, cols, TILE):
            end = min(at + TILE, cols)
            pair = [block[i, at:end, :] if other is None else block[i, at:end, :] + other[i, at:end, :] for i in (0, 1)]
            term = dot(rows_ref[:, :tok], pair[0], NT) + dot(rows_ref[:, tok:], pair[1], NT)
            parts = [term[s * share : (s + 1) * share] for s in range(4)]
            keep[:, at:end] = parts[0]
            near[:, at:end] = parts[3 - first]
            send[:, at:end] = parts[first].astype(jnp.bfloat16)
            send[:, cols + at : cols + end] = parts[3].astype(jnp.bfloat16)


def make_terms(rows, blocks, orders, waiting, others=()):
    share = rows.shape[0] // 4
    flat = [x for group in waiting for x in group]
    whole = lambda x: pl.BlockSpec(x.shape, lambda i: (0,) * len(x.shape))
    shapes = []
    for block in blocks:
        cols = block.shape[1]
        shapes += [jax.ShapeDtypeStruct((share, cols), jnp.float32)] * 2
        shapes.append(jax.ShapeDtypeStruct((share, 2 * cols), jnp.bfloat16))
    for keep, _, _ in waiting:
        shapes += [jax.ShapeDtypeStruct(keep.shape, jnp.float32), jax.ShapeDtypeStruct(keep.shape, jnp.bfloat16)]
    out = pl.pallas_call(
        functools.partial(terms_kernel, orders, len(waiting), len(others) > 0),
        grid=(1,),
        in_specs=[whole(x) for x in (rows, *others, *blocks, *flat)],
        out_specs=[whole(x) for x in shapes],
        out_shape=shapes,
        compiler_params=pltpu.CompilerParams(vmem_limit_bytes=VMEM_LIMIT),
        cost_estimate=CHEAP,
        name="weight_terms",
    )(rows, *others, *blocks, *flat)
    cut = 3 * len(blocks)
    return [list(out[n : n + 3]) for n in range(0, cut, 3)], [list(out[n : n + 2]) for n in range(cut, len(out), 2)]


def close_kernel(groups, core_ref, from_low_ref, *refs):
    owns, highs, (keep_ref, send_ref) = refs[:groups], refs[groups : 2 * groups], refs[2 * groups :]
    half = from_low_ref.shape[2]

    def write(low_ref, high_ref):
        for part in range(2):
            scale = LOGIT_SCALE if part == 0 else 1.0
            for g in range(groups):
                low = owns[g][part, 0, :half] * scale + from_low_ref[part, g].astype(jnp.float32)
                high = owns[g][part, 0, half:] * scale + highs[g][part, 0].astype(jnp.float32)
                low_ref[part, g] = low.astype(jnp.bfloat16)
                high_ref[part, g] = high.astype(jnp.bfloat16)

    @pl.when(core_ref[0] == 0)
    def _():
        write(keep_ref, send_ref)

    @pl.when(core_ref[0] == 1)
    def _():
        write(send_ref, keep_ref)


def close_sums(core, from_low, owns, highs):
    whole = lambda x: pl.BlockSpec(x.shape, lambda i, c: (0,) * x.ndim)
    out = jax.ShapeDtypeStruct(from_low.shape, jnp.bfloat16)
    return pl.pallas_call(
        functools.partial(close_kernel, len(owns)),
        grid_spec=pltpu.PrefetchScalarGridSpec(
            num_scalar_prefetch=1,
            grid=(1,),
            in_specs=[whole(x) for x in (from_low, *owns, *highs)],
            out_specs=[whole(out), whole(out)],
        ),
        out_shape=[out, out],
        compiler_params=pltpu.CompilerParams(vmem_limit_bytes=VMEM_LIMIT),
        cost_estimate=CHEAP,
        name="close_sums",
    )(core, from_low, *owns, *highs)


def place_kernel(where_ref, knocked_ref, start_ref, keep_ref, taken_ref, key_ref, value_ref, patch_ref):
    groups, tok, head_size = keep_ref.shape[1:]
    core, row_start = where_ref[0], where_ref[1]
    positions = row_start + lax.broadcasted_iota(jnp.int32, (tok, head_size), 0)
    for head in range(2 * groups):
        own = core == head // groups
        at = slice(head * head_size, (head + 1) * head_size)
        both = [
            jnp.where(own, keep_ref[part, head % groups].astype(jnp.float32), taken_ref[part, head % groups].astype(jnp.float32))
            for part in range(2)
        ]
        chosen = jnp.logical_and(knocked_ref[head] == 1, positions >= start_ref[head])
        key_ref[:, at] = jnp.where(chosen, 0.0, both[0]).astype(jnp.bfloat16)
        patch_ref[:, at] = jnp.where(chosen, both[0], 0.0).astype(jnp.bfloat16)
        value_ref[:, at] = both[1].astype(jnp.bfloat16)


def place_sums(where, knocked, patch_start, keep, taken):
    _, groups, tok, head_size = keep.shape
    whole = pl.BlockSpec(keep.shape, lambda i, *_: (0, 0, 0, 0))
    shape = (tok, 2 * groups * head_size)
    return pl.pallas_call(
        place_kernel,
        grid_spec=pltpu.PrefetchScalarGridSpec(
            num_scalar_prefetch=3,
            grid=(1,),
            in_specs=[whole, whole],
            out_specs=[pl.BlockSpec(shape, lambda i, *_: (0, 0))] * 3,
        ),
        out_shape=[jax.ShapeDtypeStruct(shape, jnp.bfloat16)] * 3,
        compiler_params=pltpu.CompilerParams(vmem_limit_bytes=VMEM_LIMIT),
        cost_estimate=CHEAP,
        name="place_sums",
    )(where, knocked, patch_start, keep, taken)


def place_terms_kernel(at_ref, *refs):
    out_ref = refs[-1]
    size = (len(refs) - 1) // 2
    cols = refs[0].shape[1]
    for n in range(size):
        for j in range(size):

            @pl.when(at_ref[n] == j)
            def _():
                out_ref[:, j * cols : (j + 1) * cols] = refs[2 * n][...] + refs[2 * n + 1][...].astype(jnp.float32)


def place_terms(at, terms):
    flat = [x for term in terms for x in term]
    share, cols = flat[0].shape
    return pl.pallas_call(
        place_terms_kernel,
        grid_spec=pltpu.PrefetchScalarGridSpec(
            num_scalar_prefetch=1,
            grid=(1,),
            in_specs=[pl.BlockSpec(x.shape, lambda i, c: (0, 0)) for x in flat],
            out_specs=pl.BlockSpec((share, cols * len(terms)), lambda i, c: (0, 0)),
        ),
        out_shape=jax.ShapeDtypeStruct((share, cols * len(terms)), jnp.float32),
        compiler_params=pltpu.CompilerParams(vmem_limit_bytes=VMEM_LIMIT),
        cost_estimate=CHEAP,
        name="place_terms",
    )(at, *flat)


def shift(shard, by):
    size = lax.axis_size("ctx")
    return lax.ppermute(shard, "ctx", [(i, i + by) for i in range(size) if 0 <= i + by < size])


def swap_cores(shard, only=None):
    size = lax.axis_size("ctx")
    return lax.ppermute(shard, "ctx", [(i, i ^ 1) for i in range(size) if only is None or i % 2 == only])


def turn(shard, by):
    size = lax.axis_size("head")
    return lax.ppermute(shard, "head", [(i, (i + by) % size) for i in range(size)])


def move(shard, pairs):
    size, n_ctx = lax.axis_size("head"), lax.axis_size("ctx")
    places = [((c + a) * size + i, (c + b) * size + j) for c in range(0, n_ctx, 2) for (a, i), (b, j) in pairs]
    return lax.ppermute(shard, ("ctx", "head"), places)


def after(values, *others):
    return lax.optimization_barrier((values, *others))[0]


def body(queries, cached_keys, values, patch_keys, out_grad, out_weight, knocked, patch_start):
    tok = queries.shape[0]
    kv_local = knocked.shape[0]
    head_size = cached_keys.shape[1] // kv_local
    cols = out_grad.shape[1]
    out_grad = out_grad.T
    n_head, n_ctx = lax.axis_size("head"), lax.axis_size("ctx")
    chips = n_ctx // 2
    place, z = lax.axis_index("ctx"), lax.axis_index("head")
    core, chip = place % 2, place // 2
    low = core == 0
    half_q, half_kv = queries.shape[1] // 2, cached_keys.shape[1] // 2
    dyn = lax.dynamic_slice_in_dim

    fast = n_head == 4 and chips == 4
    partner = swap_cores(out_grad)
    own_block = jnp.stack([jnp.where(low, out_grad, partner), jnp.where(low, partner, out_grad)])
    if fast:
        up, down = [((0, i), (0, (i + 1) % 4)) for i in range(4)], [((1, i), (1, (i - 1) % 4)) for i in range(4)]
        direct = move(own_block, up + down)
        order = [0, jnp.where(low, 3, 1), jnp.where(low, 1, 3), 2]
    else:
        direct = [turn(own_block, s) for s in range(1, n_head)]
        order = [(n_head - s) % n_head for s in range(n_head)]

    positions = place * tok + jnp.arange(tok, dtype=jnp.int32)
    chosen = (jnp.repeat(knocked, head_size)[None, :] == 1) & (
        positions[:, None] >= jnp.repeat(patch_start, head_size)[None, :]
    )
    patched = jnp.where(chosen, patch_keys, cached_keys)

    def packet_of(which):
        return jnp.concatenate(
            [
                dyn(queries, which * half_q, half_q, 1),
                dyn(patched, which * half_kv, half_kv, 1),
                dyn(values, which * half_kv, half_kv, 1),
            ],
            axis=1,
        )

    mine, other = packet_of(core), swap_cores(packet_of(1 - core))
    packet = jnp.concatenate([jnp.where(low, mine, other), jnp.where(low, other, mine)], axis=0)
    before = shift(packet[:, half_q:], 2)

    weight_half = dyn(out_weight, core * half_q, half_q, 0)
    weights = [dyn(weight_half, ((z + d) % n_head) * cols, cols, 1) for d in order]
    core_id = core[None].astype(jnp.int32)
    grads = add_grads([own_block], weights[:1], None, jnp.float32)
    before = after(before, grads, weights)

    attention, attended = forward(chip[None].astype(jnp.int32), packet, before, head_size)
    if fast:
        share = out_weight.shape[0] // n_ctx
        parity = attended.reshape(chips // 2, 2, share, 2 * tok)
        kept, given = dyn(parity, core, 1, 1)[:, 0], dyn(parity, 1 - core, 1, 1)[:, 0]
        taken = swap_cores(given)
        by_chip = jnp.concatenate([jnp.where(low, kept, taken), jnp.where(low, taken, kept)], axis=0)
        by_distance = jnp.concatenate([dyn(by_chip, chip ^ s, 1, 0) for s in range(chips)], axis=0)
        by_distance = by_distance.reshape(chips * share, 2 * tok)

        def exchange(shard, distance):
            return lax.ppermute(shard, "ctx", [(i, i ^ (2 * distance)) for i in range(n_ctx)])

        direct = after(direct, by_distance)
        final = move(direct, [((i % 2, i), (i % 2, j)) for i, j in [(0, 1), (1, 0), (2, 3), (3, 2)]])
        blocks = [direct, swap_cores(direct)]
        (own_terms, up_terms, down_terms), _ = make_terms(by_distance, [own_block, *blocks], (1, 1, 2), [])
        own_got, up_got, down_got = exchange(own_terms[2], 1), exchange(up_terms[2], 1), exchange(down_terms[2], 2)
        grads = add_grads(blocks, weights[1:3], grads, jnp.float32)

        final, own_got, down_got, grads = lax.optimization_barrier((final, own_got, down_got, grads))
        there = swap_cores(final)
        (last_terms,), (own_sum, down_sum) = make_terms(
            by_distance, [final], (2,), [(*own_terms[:2], own_got), (*down_terms[:2], down_got)], [there]
        )
        last_got = exchange(last_terms[2], 2)
        own_sum[1], down_sum[1] = exchange(own_sum[1], 2), exchange(down_sum[1], 1)
        final, there, _, up_got = lax.optimization_barrier((final, there, last_terms[2], up_got))
        grads = add_grads([final], weights[3:], grads, jnp.bfloat16, [there])
    else:
        blocks = [own_block, *direct]
        grads = add_grads(blocks[1:], weights[1:], grads, jnp.float32).astype(jnp.bfloat16)
        term = jnp.stack([sum(dot(attended[:, i * tok : (i + 1) * tok], x[i], NT) for i in (0, 1)) for x in blocks])
        term = jnp.concatenate([dyn(term, (z - j) % n_head, 1, 0)[0] for j in range(n_head)], axis=1)
        term = jnp.concatenate([jnp.where(low, term, 0.0), jnp.where(low, 0.0, term)], axis=0)
        weight_grad = lax.psum_scatter(term, "ctx", scatter_dimension=0, tiled=True)
    all_groups = (0, packet.shape[1] // (4 * head_size))
    query_low, prev_low, carry = backward(0, all_groups, packet, before, attention, grads, None, head_size)
    if fast:
        sent = (own_sum[1], down_sum[1])
        query_low, prev_low, carry, last_got, sent = lax.optimization_barrier(
            (query_low, prev_low, carry, last_got, sent)
        )
        own_sum[1], down_sum[1] = sent
        waiting = [(*up_terms[:2], up_got), (*last_terms[:2], last_got)]
        _, (up_sum, last_sum) = make_terms(by_distance, [], (), waiting)
        prev_low = after(prev_low, last_sum[1])
        up_sum[1], last_sum[1] = exchange(up_sum[1], 2), exchange(last_sum[1], 1)
    from_low = shift(prev_low, -2)
    parts, from_high = [], []
    for g in range(all_groups[1]):
        part = backward(1, (g, 1), packet, before, attention, grads, carry, head_size)
        if g > 0:
            part, from_low, from_high = lax.optimization_barrier((part, from_low, from_high))
        parts.append(part)
        from_high.append(shift(part[1], -2))
    query_high = jnp.concatenate([part[0] for part in parts], axis=1)

    if fast:
        at = jnp.stack([(z + d) % n_head for d in order]).astype(jnp.int32)
        weight_grad = place_terms(at, [own_sum, up_sum, down_sum, last_sum])

    query_kept = jnp.where(low, query_low, query_high)
    query_taken = swap_cores(jnp.where(low, query_high, query_low))
    query_grad = jnp.concatenate(
        [jnp.where(low, query_kept, query_taken), jnp.where(low, query_taken, query_kept)], axis=1
    )
    from_high = after(from_high, weight_grad)
    keep, send = close_sums(core_id, from_low, [part[2] for part in parts], from_high)
    rows_at = jnp.stack([core, place * tok]).astype(jnp.int32)
    taken = after(swap_cores(send), query_grad)
    key_grad, value_grad, patch_grad = place_sums(rows_at, knocked, patch_start, keep, taken)
    return (query_grad, key_grad, value_grad, patch_grad, weight_grad)


def solution(mesh):
    split = P("ctx", "head")
    return jax.shard_map(
        body,
        mesh=mesh,
        in_specs=(split, split, split, split, split, P("head", None), P("head"), P("head")),
        out_specs=(split, split, split, split, P(("head", "ctx"), None)),
        check_vma=False,
    )
```

```python
import functools

import jax
import jax.numpy as jnp
from jax import lax
from jax.experimental import pallas as pl
from jax.experimental.pallas import tpu as pltpu
from jax.sharding import PartitionSpec as P

LOGIT_SCALE = 168.0 ** (-0.5)
EXP2_SCALE = LOGIT_SCALE * 1.4426950408889634
TILE = 256
VMEM_LIMIT = 24 * 1024 * 1024
ATTENTION_VMEM_LIMIT = 48 * 1024 * 1024
CHEAP = pl.CostEstimate(flops=1, bytes_accessed=1, transcendentals=0)

NT = (((1,), (1,)), ((), ()))
NN = (((1,), (0,)), ((), ()))


def dot(a, b, dims=NN):
    return lax.dot_general(a, b, dims, preferred_element_type=jnp.float32)


def stack_heads(pair, head_size):
    return jnp.concatenate([pair[:, :head_size], pair[:, head_size:]], axis=0)


def forward_kernel(chip_ref, q_ref, k_ref, v_ref, pk_ref, pv_ref, p_ref, at_ref, keys, values_t):
    tile = pl.program_id(1)
    rows, head_size = k_ref.shape
    blocks = rows // TILE

    @pl.when(tile == 0)
    def _():
        keys[:rows] = pk_ref[...]
        keys[rows:] = k_ref[...]
        values_t[:, :rows] = pv_ref[...].T
        values_t[:, rows:] = v_ref[...].T

    q = stack_heads(q_ref[...], head_size)
    key_id = lax.broadcasted_iota(jnp.int32, (TILE, 2 * TILE), 0)
    query_id = lax.broadcasted_iota(jnp.int32, (TILE, 2 * TILE), 1) & (TILE - 1)
    first = chip_ref[0] == 0
    top = None
    for b in range(blocks + 1):
        start = pl.multiple_of((tile + b) * TILE, TILE)
        s = dot(keys[pl.ds(start, TILE), :], q, NT)
        if b == 0:
            s = jnp.where(key_id > query_id, s, -jnp.inf)
        if b == blocks:
            s = jnp.where(key_id <= query_id, s, -jnp.inf)
        else:
            s = s + jnp.where(jnp.logical_and(first, tile + b < blocks), -jnp.inf, 0.0)
        p_ref[0, 0, b * TILE : (b + 1) * TILE, :] = s
        here = jnp.max(s, axis=0, keepdims=True)
        top = here if top is None else jnp.maximum(top, here)
    total = None
    for b in range(blocks + 1):
        part = pl.ds(b * TILE, TILE)
        e = jnp.exp2((p_ref[0, 0, part, :] - top) * EXP2_SCALE)
        p_ref[0, 0, part, :] = e
        here = jnp.sum(e, axis=0, keepdims=True)
        total = here if total is None else total + here
    inverse = 1.0 / total
    out = None
    for b in range(blocks + 1):
        part = pl.ds(b * TILE, TILE)
        start = pl.multiple_of((tile + b) * TILE, TILE)
        p = p_ref[0, 0, part, :] * inverse
        p_ref[0, 0, part, :] = p
        term = dot(values_t[:, pl.ds(start, TILE)], p.astype(jnp.bfloat16))
        out = term if out is None else out + term
    at_ref[:head_size] = out[:, :TILE].astype(jnp.bfloat16)
    at_ref[head_size:] = out[:, TILE:].astype(jnp.bfloat16)


def forward(chip, packet, before, head_size):
    rows = packet.shape[0]
    groups = packet.shape[1] // (4 * head_size)
    tiles = rows // TILE
    span = rows + TILE
    grid_spec = pltpu.PrefetchScalarGridSpec(
        num_scalar_prefetch=1,
        grid=(groups, tiles),
        in_specs=[
            pl.BlockSpec((TILE, 2 * head_size), lambda g, i, c: (i, g)),
            pl.BlockSpec((rows, head_size), lambda g, i, c: (0, 2 * groups + g)),
            pl.BlockSpec((rows, head_size), lambda g, i, c: (0, 3 * groups + g)),
            pl.BlockSpec((rows, head_size), lambda g, i, c: (0, g)),
            pl.BlockSpec((rows, head_size), lambda g, i, c: (0, groups + g)),
        ],
        out_specs=[
            pl.BlockSpec((1, 1, span, 2 * TILE), lambda g, i, c: (g, i, 0, 0)),
            pl.BlockSpec((2 * head_size, TILE), lambda g, i, c: (g, i)),
        ],
        scratch_shapes=[
            pltpu.VMEM((2 * rows, head_size), jnp.bfloat16),
            pltpu.VMEM((head_size, 2 * rows), jnp.bfloat16),
        ],
    )
    return pl.pallas_call(
        forward_kernel,
        grid_spec=grid_spec,
        out_shape=[
            jax.ShapeDtypeStruct((groups, tiles, span, 2 * TILE), jnp.float32),
            jax.ShapeDtypeStruct((groups * 2 * head_size, rows), jnp.bfloat16),
        ],
        compiler_params=pltpu.CompilerParams(vmem_limit_bytes=ATTENTION_VMEM_LIMIT),
        cost_estimate=CHEAP,
        name="attention_forward",
    )(chip, packet, packet, packet, before, before)


def backward_kernel(
    phase, q_ref, k_ref, v_ref, pk_ref, pv_ref, p_ref, do_ref, carry_ref, dq_ref, dprev_ref, keep_ref, keys_t, values, dk, dv, dp
):
    tile = pl.program_id(1)
    rows, head_size = k_ref.shape
    blocks = rows // TILE
    half = rows // 2
    old = rows - phase * half

    @pl.when(tile == 0)
    def _():
        keys_t[:, :old] = pk_ref[rows - old :, :].T
        keys_t[:, old:] = k_ref[: half + rows - old, :].T
        values[:old] = pv_ref[rows - old :, :]
        values[old:] = v_ref[: half + rows - old, :]
        if phase == 0:
            dk[...] = jnp.zeros_like(dk)
            dv[...] = jnp.zeros_like(dv)
        else:
            dk[:rows] = carry_ref[0, 0]
            dv[:rows] = carry_ref[1, 0]
            dk[rows:] = jnp.zeros((half, head_size), jnp.float32)
            dv[rows:] = jnp.zeros((half, head_size), jnp.float32)

    q = stack_heads(q_ref[...], head_size)
    do = jnp.concatenate([do_ref[:head_size], do_ref[head_size:]], axis=1)
    centre = None
    for b in range(blocks + 1):
        start = pl.multiple_of((tile + b) * TILE, TILE)
        part = pl.ds(b * TILE, TILE)
        p = p_ref[0, 0, part, :]
        grad = dot(values[pl.ds(start, TILE), :], do)
        dp[part, :] = grad
        here = jnp.sum(p * grad, axis=0, keepdims=True)
        centre = here if centre is None else centre + here
        dv[pl.ds(start, TILE), :] += dot(p.astype(jnp.bfloat16), do, NT)
    out = None
    for b in range(blocks + 1):
        start = pl.multiple_of((tile + b) * TILE, TILE)
        part = pl.ds(b * TILE, TILE)
        ds = (p_ref[0, 0, part, :] * (dp[part, :] - centre)).astype(jnp.bfloat16)
        dk[pl.ds(start, TILE), :] += dot(ds, q)
        term = dot(keys_t[:, pl.ds(start, TILE)], ds)
        out = term if out is None else out + term
    out = out * LOGIT_SCALE
    dq_ref[:, :head_size] = out[:, :TILE].T.astype(jnp.bfloat16)
    dq_ref[:, head_size:] = out[:, TILE:].T.astype(jnp.bfloat16)

    @pl.when(tile == pl.num_programs(1) - 1)
    def _():
        dprev_ref[0, 0] = (dk[:half] * LOGIT_SCALE).astype(jnp.bfloat16)
        dprev_ref[1, 0] = dv[:half].astype(jnp.bfloat16)
        keep_ref[0, 0] = dk[half:]
        keep_ref[1, 0] = dv[half:]


def backward(phase, members, packet, before, attention, out_grads, carry, head_size):
    rows = packet.shape[0]
    groups = packet.shape[1] // (4 * head_size)
    g0, count = members
    tiles = rows // TILE // 2
    half = rows // 2
    span = rows + TILE
    first = phase * tiles
    if carry is None:
        carry = jnp.zeros((2, 1, 8, head_size), jnp.float32)
        carry_spec = pl.BlockSpec((2, 1, 8, head_size), lambda g, i: (0, 0, 0, 0))
    else:
        carry_spec = pl.BlockSpec((2, 1, rows, head_size), lambda g, i: (0, g0 + g, 0, 0))
    return pl.pallas_call(
        functools.partial(backward_kernel, phase),
        grid=(count, tiles),
        in_specs=[
            pl.BlockSpec((TILE, 2 * head_size), lambda g, i: (first + i, g0 + g)),
            pl.BlockSpec((rows, head_size), lambda g, i: (0, 2 * groups + g0 + g)),
            pl.BlockSpec((rows, head_size), lambda g, i: (0, 3 * groups + g0 + g)),
            pl.BlockSpec((rows, head_size), lambda g, i: (0, g0 + g)),
            pl.BlockSpec((rows, head_size), lambda g, i: (0, groups + g0 + g)),
            pl.BlockSpec((1, 1, span, 2 * TILE), lambda g, i: (g0 + g, first + i, 0, 0)),
            pl.BlockSpec((2 * head_size, TILE), lambda g, i: (g0 + g, first + i)),
            carry_spec,
        ],
        out_specs=[
            pl.BlockSpec((TILE, 2 * head_size), lambda g, i: (i, g)),
            pl.BlockSpec((2, 1, half, head_size), lambda g, i: (0, g, 0, 0)),
            pl.BlockSpec((2, 1, rows, head_size), lambda g, i: (0, g, 0, 0)),
        ],
        out_shape=[
            jax.ShapeDtypeStruct((half, count * 2 * head_size), jnp.bfloat16),
            jax.ShapeDtypeStruct((2, count, half, head_size), jnp.bfloat16),
            jax.ShapeDtypeStruct((2, count, rows, head_size), jnp.float32),
        ],
        scratch_shapes=[
            pltpu.VMEM((head_size, rows + half), jnp.bfloat16),
            pltpu.VMEM((rows + half, head_size), jnp.bfloat16),
            pltpu.VMEM((rows + half, head_size), jnp.float32),
            pltpu.VMEM((rows + half, head_size), jnp.float32),
            pltpu.VMEM((span, 2 * TILE), jnp.float32),
        ],
        compiler_params=pltpu.CompilerParams(vmem_limit_bytes=ATTENTION_VMEM_LIMIT),
        cost_estimate=CHEAP,
        name="attention_backward",
    )(packet, packet, packet, before, before, attention, out_grads, carry)


def grads_kernel(number, halves, *refs):
    blocks, weights = refs[:number], refs[number : 2 * number]
    total = None
    others = refs[2 * number : 3 * number] if halves else [None] * number
    for block, other, weight in zip(blocks, others, weights):
        term = dot(weight[...], block[0] if other is None else block[0] + other[0])
        total = term if total is None else total + term
    for old in refs[(3 if halves else 2) * number : -1]:
        total = total + old[...]
    refs[-1][...] = total.astype(refs[-1].dtype)


def add_grads(blocks, weights, total, dtype, others=()):
    _, cols, tok = blocks[0].shape
    width = weights[0].shape[0]
    tiles = tok // TILE
    tile_spec = pl.BlockSpec((width, TILE), lambda i: (0, i))
    number = len(blocks)
    return pl.pallas_call(
        functools.partial(grads_kernel, number, len(others) > 0),
        grid=(2 * tiles,),
        in_specs=[pl.BlockSpec((1, cols, TILE), lambda i: (i // tiles, 0, i % tiles))] * number
        + [pl.BlockSpec((width, cols), lambda i: (0, 0))] * number
        + [pl.BlockSpec((1, cols, TILE), lambda i: (i // tiles, 0, i % tiles))] * len(others)
        + ([] if total is None else [tile_spec]),
        out_specs=tile_spec,
        out_shape=jax.ShapeDtypeStruct((width, 2 * tok), dtype),
        compiler_params=pltpu.CompilerParams(vmem_limit_bytes=VMEM_LIMIT),
        cost_estimate=CHEAP,
        name="out_grads",
    )(*blocks, *weights, *others, *([] if total is None else [total]))


def terms_kernel(orders, count, halves, rows_ref, *refs):
    number = len(orders)
    others, refs = (refs[:number], refs[number:]) if halves else ([None] * number, refs)
    blocks, waiting = refs[:number], refs[number : number + 3 * count]
    outs, passed = refs[number + 3 * count : number + 3 * count + 3 * number], refs[number + 3 * count + 3 * number :]
    for n in range(count):
        keep, near, got = waiting[3 * n : 3 * n + 3]
        cols = keep.shape[1]
        passed[2 * n][...] = keep[...] + got[:, :cols].astype(jnp.float32)
        passed[2 * n + 1][...] = (near[...] + got[:, cols:].astype(jnp.float32)).astype(jnp.bfloat16)
    for n, (block, other, first) in enumerate(zip(blocks, others, orders)):
        _, cols, tok = block.shape
        share = rows_ref.shape[0] // 4
        keep, near, send = outs[3 * n : 3 * n + 3]
        for at in range(0, cols, TILE):
            end = min(at + TILE, cols)
            pair = [block[i, at:end, :] if other is None else block[i, at:end, :] + other[i, at:end, :] for i in (0, 1)]
            term = dot(rows_ref[:, :tok], pair[0], NT) + dot(rows_ref[:, tok:], pair[1], NT)
            parts = [term[s * share : (s + 1) * share] for s in range(4)]
            keep[:, at:end] = parts[0]
            near[:, at:end] = parts[3 - first]
            send[:, at:end] = parts[first].astype(jnp.bfloat16)
            send[:, cols + at : cols + end] = parts[3].astype(jnp.bfloat16)


def make_terms(rows, blocks, orders, waiting, others=()):
    share = rows.shape[0] // 4
    flat = [x for group in waiting for x in group]
    whole = lambda x: pl.BlockSpec(x.shape, lambda i: (0,) * len(x.shape))
    shapes = []
    for block in blocks:
        cols = block.shape[1]
        shapes += [jax.ShapeDtypeStruct((share, cols), jnp.float32)] * 2
        shapes.append(jax.ShapeDtypeStruct((share, 2 * cols), jnp.bfloat16))
    for keep, _, _ in waiting:
        shapes += [jax.ShapeDtypeStruct(keep.shape, jnp.float32), jax.ShapeDtypeStruct(keep.shape, jnp.bfloat16)]
    out = pl.pallas_call(
        functools.partial(terms_kernel, orders, len(waiting), len(others) > 0),
        grid=(1,),
        in_specs=[whole(x) for x in (rows, *others, *blocks, *flat)],
        out_specs=[whole(x) for x in shapes],
        out_shape=shapes,
        compiler_params=pltpu.CompilerParams(vmem_limit_bytes=VMEM_LIMIT),
        cost_estimate=CHEAP,
        name="weight_terms",
    )(rows, *others, *blocks, *flat)
    cut = 3 * len(blocks)
    return [list(out[n : n + 3]) for n in range(0, cut, 3)], [list(out[n : n + 2]) for n in range(cut, len(out), 2)]


def close_kernel(groups, core_ref, from_low_ref, *refs):
    owns, highs, (keep_ref, send_ref) = refs[:groups], refs[groups : 2 * groups], refs[2 * groups :]
    half = from_low_ref.shape[2]

    def write(low_ref, high_ref):
        for part in range(2):
            scale = LOGIT_SCALE if part == 0 else 1.0
            for g in range(groups):
                low = owns[g][part, 0, :half] * scale + from_low_ref[part, g].astype(jnp.float32)
                high = owns[g][part, 0, half:] * scale + highs[g][part, 0].astype(jnp.float32)
                low_ref[part, g] = low.astype(jnp.bfloat16)
                high_ref[part, g] = high.astype(jnp.bfloat16)

    @pl.when(core_ref[0] == 0)
    def _():
        write(keep_ref, send_ref)

    @pl.when(core_ref[0] == 1)
    def _():
        write(send_ref, keep_ref)


def close_sums(core, from_low, owns, highs):
    whole = lambda x: pl.BlockSpec(x.shape, lambda i, c: (0,) * x.ndim)
    out = jax.ShapeDtypeStruct(from_low.shape, jnp.bfloat16)
    return pl.pallas_call(
        functools.partial(close_kernel, len(owns)),
        grid_spec=pltpu.PrefetchScalarGridSpec(
            num_scalar_prefetch=1,
            grid=(1,),
            in_specs=[whole(x) for x in (from_low, *owns, *highs)],
            out_specs=[whole(out), whole(out)],
        ),
        out_shape=[out, out],
        compiler_params=pltpu.CompilerParams(vmem_limit_bytes=VMEM_LIMIT),
        cost_estimate=CHEAP,
        name="close_sums",
    )(core, from_low, *owns, *highs)


def place_kernel(where_ref, knocked_ref, start_ref, keep_ref, taken_ref, key_ref, value_ref, patch_ref):
    groups, tok, head_size = keep_ref.shape[1:]
    core, row_start = where_ref[0], where_ref[1]
    positions = row_start + lax.broadcasted_iota(jnp.int32, (tok, head_size), 0)
    for head in range(2 * groups):
        own = core == head // groups
        at = slice(head * head_size, (head + 1) * head_size)
        both = [
            jnp.where(own, keep_ref[part, head % groups].astype(jnp.float32), taken_ref[part, head % groups].astype(jnp.float32))
            for part in range(2)
        ]
        chosen = jnp.logical_and(knocked_ref[head] == 1, positions >= start_ref[head])
        key_ref[:, at] = jnp.where(chosen, 0.0, both[0]).astype(jnp.bfloat16)
        patch_ref[:, at] = jnp.where(chosen, both[0], 0.0).astype(jnp.bfloat16)
        value_ref[:, at] = both[1].astype(jnp.bfloat16)


def place_sums(where, knocked, patch_start, keep, taken):
    _, groups, tok, head_size = keep.shape
    whole = pl.BlockSpec(keep.shape, lambda i, *_: (0, 0, 0, 0))
    shape = (tok, 2 * groups * head_size)
    return pl.pallas_call(
        place_kernel,
        grid_spec=pltpu.PrefetchScalarGridSpec(
            num_scalar_prefetch=3,
            grid=(1,),
            in_specs=[whole, whole],
            out_specs=[pl.BlockSpec(shape, lambda i, *_: (0, 0))] * 3,
        ),
        out_shape=[jax.ShapeDtypeStruct(shape, jnp.bfloat16)] * 3,
        compiler_params=pltpu.CompilerParams(vmem_limit_bytes=VMEM_LIMIT),
        cost_estimate=CHEAP,
        name="place_sums",
    )(where, knocked, patch_start, keep, taken)


def place_terms_kernel(at_ref, *refs):
    out_ref = refs[-1]
    size = (len(refs) - 1) // 2
    cols = refs[0].shape[1]
    for n in range(size):
        for j in range(size):

            @pl.when(at_ref[n] == j)
            def _():
                out_ref[:, j * cols : (j + 1) * cols] = refs[2 * n][...] + refs[2 * n + 1][...].astype(jnp.float32)


def place_terms(at, terms):
    flat = [x for term in terms for x in term]
    share, cols = flat[0].shape
    return pl.pallas_call(
        place_terms_kernel,
        grid_spec=pltpu.PrefetchScalarGridSpec(
            num_scalar_prefetch=1,
            grid=(1,),
            in_specs=[pl.BlockSpec(x.shape, lambda i, c: (0, 0)) for x in flat],
            out_specs=pl.BlockSpec((share, cols * len(terms)), lambda i, c: (0, 0)),
        ),
        out_shape=jax.ShapeDtypeStruct((share, cols * len(terms)), jnp.float32),
        compiler_params=pltpu.CompilerParams(vmem_limit_bytes=VMEM_LIMIT),
        cost_estimate=CHEAP,
        name="place_terms",
    )(at, *flat)


def shift(shard, by):
    size = lax.axis_size("ctx")
    return lax.ppermute(shard, "ctx", [(i, i + by) for i in range(size) if 0 <= i + by < size])


def swap_cores(shard, only=None):
    size = lax.axis_size("ctx")
    return lax.ppermute(shard, "ctx", [(i, i ^ 1) for i in range(size) if only is None or i % 2 == only])


def turn(shard, by):
    size = lax.axis_size("head")
    return lax.ppermute(shard, "head", [(i, (i + by) % size) for i in range(size)])


def move(shard, pairs):
    size, n_ctx = lax.axis_size("head"), lax.axis_size("ctx")
    places = [((c + a) * size + i, (c + b) * size + j) for c in range(0, n_ctx, 2) for (a, i), (b, j) in pairs]
    return lax.ppermute(shard, ("ctx", "head"), places)


def after(values, *others):
    return lax.optimization_barrier((values, *others))[0]


def body(queries, cached_keys, values, patch_keys, out_grad, out_weight, knocked, patch_start):
    tok = queries.shape[0]
    kv_local = knocked.shape[0]
    head_size = cached_keys.shape[1] // kv_local
    cols = out_grad.shape[1]
    out_grad = out_grad.T
    n_head, n_ctx = lax.axis_size("head"), lax.axis_size("ctx")
    chips = n_ctx // 2
    place, z = lax.axis_index("ctx"), lax.axis_index("head")
    core, chip = place % 2, place // 2
    low = core == 0
    half_q, half_kv = queries.shape[1] // 2, cached_keys.shape[1] // 2
    dyn = lax.dynamic_slice_in_dim

    fast = n_head == 4 and chips == 4
    partner = swap_cores(out_grad)
    own_block = jnp.stack([jnp.where(low, out_grad, partner), jnp.where(low, partner, out_grad)])
    if fast:
        up, down = [((0, i), (0, (i + 1) % 4)) for i in range(4)], [((1, i), (1, (i - 1) % 4)) for i in range(4)]
        direct = move(own_block, up + down)
        order = [0, jnp.where(low, 3, 1), jnp.where(low, 1, 3), 2]
    else:
        direct = [turn(own_block, s) for s in range(1, n_head)]
        order = [(n_head - s) % n_head for s in range(n_head)]

    positions = place * tok + jnp.arange(tok, dtype=jnp.int32)
    chosen = (jnp.repeat(knocked, head_size)[None, :] == 1) & (
        positions[:, None] >= jnp.repeat(patch_start, head_size)[None, :]
    )
    patched = jnp.where(chosen, patch_keys, cached_keys)

    def packet_of(which):
        return jnp.concatenate(
            [
                dyn(queries, which * half_q, half_q, 1),
                dyn(patched, which * half_kv, half_kv, 1),
                dyn(values, which * half_kv, half_kv, 1),
            ],
            axis=1,
        )

    mine, other = packet_of(core), swap_cores(packet_of(1 - core))
    packet = jnp.concatenate([jnp.where(low, mine, other), jnp.where(low, other, mine)], axis=0)
    before = shift(packet[:, half_q:], 2)

    weight_half = dyn(out_weight, core * half_q, half_q, 0)
    weights = [dyn(weight_half, ((z + d) % n_head) * cols, cols, 1) for d in order]
    core_id = core[None].astype(jnp.int32)
    grads = add_grads([own_block], weights[:1], None, jnp.float32)
    before = after(before, grads, weights)

    attention, attended = forward(chip[None].astype(jnp.int32), packet, before, head_size)
    if fast:
        share = out_weight.shape[0] // n_ctx
        parity = attended.reshape(chips // 2, 2, share, 2 * tok)
        kept, given = dyn(parity, core, 1, 1)[:, 0], dyn(parity, 1 - core, 1, 1)[:, 0]
        taken = swap_cores(given)
        by_chip = jnp.concatenate([jnp.where(low, kept, taken), jnp.where(low, taken, kept)], axis=0)
        by_distance = jnp.concatenate([dyn(by_chip, chip ^ s, 1, 0) for s in range(chips)], axis=0)
        by_distance = by_distance.reshape(chips * share, 2 * tok)

        def exchange(shard, distance):
            return lax.ppermute(shard, "ctx", [(i, i ^ (2 * distance)) for i in range(n_ctx)])

        direct = after(direct, by_distance)
        final = move(direct, [((i % 2, i), (i % 2, j)) for i, j in [(0, 1), (1, 0), (2, 3), (3, 2)]])
        blocks = [direct, swap_cores(direct)]
        (own_terms, up_terms, down_terms), _ = make_terms(by_distance, [own_block, *blocks], (1, 1, 2), [])
        own_got, up_got, down_got = exchange(own_terms[2], 1), exchange(up_terms[2], 1), exchange(down_terms[2], 2)
        grads = add_grads(blocks, weights[1:3], grads, jnp.float32)

        final, own_got, down_got, grads = lax.optimization_barrier((final, own_got, down_got, grads))
        there = swap_cores(final)
        (last_terms,), (own_sum, down_sum) = make_terms(
            by_distance, [final], (2,), [(*own_terms[:2], own_got), (*down_terms[:2], down_got)], [there]
        )
        last_got = exchange(last_terms[2], 2)
        own_sum[1], down_sum[1] = exchange(own_sum[1], 2), exchange(down_sum[1], 1)
        final, there, _, up_got = lax.optimization_barrier((final, there, last_terms[2], up_got))
        grads = add_grads([final], weights[3:], grads, jnp.bfloat16, [there])
    else:
        blocks = [own_block, *direct]
        grads = add_grads(blocks[1:], weights[1:], grads, jnp.float32).astype(jnp.bfloat16)
        term = jnp.stack([sum(dot(attended[:, i * tok : (i + 1) * tok], x[i], NT) for i in (0, 1)) for x in blocks])
        term = jnp.concatenate([dyn(term, (z - j) % n_head, 1, 0)[0] for j in range(n_head)], axis=1)
        term = jnp.concatenate([jnp.where(low, term, 0.0), jnp.where(low, 0.0, term)], axis=0)
        weight_grad = lax.psum_scatter(term, "ctx", scatter_dimension=0, tiled=True)
    all_groups = (0, packet.shape[1] // (4 * head_size))
    query_low, prev_low, carry = backward(0, all_groups, packet, before, attention, grads, None, head_size)
    if fast:
        sent = (own_sum[1], down_sum[1])
        query_low, prev_low, carry, last_got, sent = lax.optimization_barrier(
            (query_low, prev_low, carry, last_got, sent)
        )
        own_sum[1], down_sum[1] = sent
        waiting = [(*up_terms[:2], up_got), (*last_terms[:2], last_got)]
        _, (up_sum, last_sum) = make_terms(by_distance, [], (), waiting)
        prev_low = after(prev_low, last_sum[1])
        up_sum[1], last_sum[1] = exchange(up_sum[1], 2), exchange(last_sum[1], 1)
    from_low = shift(prev_low, -2)
    parts, from_high = [], []
    for g in range(all_groups[1]):
        part = backward(1, (g, 1), packet, before, attention, grads, carry, head_size)
        if g > 0:
            part, from_low = lax.optimization_barrier((part, from_low))
        parts.append(part)
        from_high.append(shift(part[1], -2))
    query_high = jnp.concatenate([part[0] for part in parts], axis=1)

    if fast:
        at = jnp.stack([(z + d) % n_head for d in order]).astype(jnp.int32)
        weight_grad = place_terms(at, [own_sum, up_sum, down_sum, last_sum])

    query_kept = jnp.where(low, query_low, query_high)
    query_taken = swap_cores(jnp.where(low, query_high, query_low))
    query_grad = jnp.concatenate(
        [jnp.where(low, query_kept, query_taken), jnp.where(low, query_taken, query_kept)], axis=1
    )
    from_high = after(from_high, weight_grad)
    keep, send = close_sums(core_id, from_low, [part[2] for part in parts], from_high)
    rows_at = jnp.stack([core, place * tok]).astype(jnp.int32)
    taken = after(swap_cores(send), query_grad)
    key_grad, value_grad, patch_grad = place_sums(rows_at, knocked, patch_start, keep, taken)
    return (query_grad, key_grad, value_grad, patch_grad, weight_grad)


def solution(mesh):
    split = P("ctx", "head")
    return jax.shard_map(
        body,
        mesh=mesh,
        in_specs=(split, split, split, split, split, P("head", None), P("head"), P("head")),
        out_specs=(split, split, split, split, P(("head", "ctx"), None)),
        check_vma=False,
    )
```
